32 devices in a mesh: tm: 16 (over z, x, core), mode: 2 (over y).
Axes of the slice: x: 2, y: 2, z: 4, core: 2. Of those that a mesh axis runs over, the one named last changes fastest.
Arguments:
- fields: float32 [16, 2, 1024, 1024], P('tm', None, 'mode'), may hold values from -2.5 to 2.5
- offsets: int32 [16, 2], P('tm'), may hold values from 1 to 4
Outputs:
- products: float32 [16, 2, 2, 1024, 1024], P('tm', None, None, 'mode')
- correlators: float32 [16, 2], P('tm')
The draws below stay inside these ranges and needn't reach their ends.
All inputs are finite; a program needn't handle non-finite values.
Results may differ from the reference program's by a relative error of at most 0.0003.
Values sent between devices are 32-bit elements; how exact they have to be, the bound alone decides.
No kernel may reach another device: no remote copies, remote signals or barrier semaphores. Data moves between devices by JAX's collectives and lax.ppermute only.
A program may use at most 128 MiB of HBM per device.

```python
import jax
import jax.numpy as jnp
from jax import lax

N = 1024
K = 2
TS = 16


def place_ends(values, own_key, smallest, largest):
    shape = values.shape
    place = [jax.random.randint(jax.random.fold_in(own_key, axis), (), 0, shape[axis]) for axis in range(len(shape))]
    values = values.at[tuple(place)].set(smallest)
    longest = shape.index(max(shape))
    place[longest] = (place[longest] + 1) % shape[longest]
    return values.at[tuple(place)].set(largest)


def level_of(stream_key, dims, cuts, smallest, high):
    loudness = 1.0
    for dim, blocks in cuts:
        heights = jax.random.uniform(jax.random.fold_in(jax.random.fold_in(stream_key, 6), dim), (blocks,), jnp.float32, smallest / len(cuts), high / len(cuts))
        loudness = loudness * jnp.repeat(jnp.exp(heights), dims[dim] // blocks).reshape((-1,) + (1,) * (len(dims) - 1 - dim))
    return loudness


def normal_values(own_key, shape, spread, limit, pieces=(), kind=jnp.bfloat16):
    entries = spread * jax.random.normal(own_key, shape, jnp.float32)
    if pieces:
        entries = entries * level_of(own_key, shape, pieces, -0.22, 0.18)
    return jnp.clip(entries, -limit, limit).astype(kind)


def setup_inputs(seed: int = 0) -> dict:
    key_list = jax.random.split(jax.random.key(seed), 3)
    fields = normal_values(key_list[0], (TS, 2, N, N), (N ** -0.25), 2.5, ((0, 16), (2, 2)), jnp.float32)
    offsets = place_ends(jax.random.randint(key_list[1], (TS, K), 1, 5), jax.random.fold_in(key_list[1], 1), 1, 4).astype(jnp.int32)
    return dict(fields=fields, offsets=offsets)


def complex_product(left, right):
    hi = lax.Precision.HIGHEST
    real = jnp.dot(left[0], right[0], precision=hi, preferred_element_type=jnp.float32) - jnp.dot(left[1], right[1], precision=hi, preferred_element_type=jnp.float32)
    imag = jnp.dot(left[0], right[1], precision=hi, preferred_element_type=jnp.float32) + jnp.dot(left[1], right[0], precision=hi, preferred_element_type=jnp.float32)
    return jnp.stack([real, imag])


def reference(fields, offsets):
    count = fields.shape[0]
    width = fields.shape[2]

    def one_pair(item):
        source = item[0]
        offset = item[1]
        sink = (source + offset) % count
        left = lax.dynamic_index_in_dim(fields, source.astype(jnp.int32), 0, keepdims=False)
        right = lax.dynamic_index_in_dim(fields, sink.astype(jnp.int32), 0, keepdims=False)
        forward = complex_product(left, right)
        partner = complex_product(right, left)
        trace = jnp.sum(forward * partner) / jnp.float32(width)
        return forward, trace

    sources = jnp.repeat(jnp.arange(count, dtype=jnp.int32), offsets.shape[1])
    items = jnp.stack([sources, offsets.reshape(-1).astype(jnp.int32)], axis=1)
    forward, trace = lax.map(one_pair, items)
    products = forward.reshape((count, offsets.shape[1]) + forward.shape[1:])
    correlators = trace.reshape(count, offsets.shape[1])
    return products, correlators
```

```python
import functools

import jax
import jax.numpy as jnp
from jax import lax
from jax.experimental import pallas as pl
from jax.experimental.pallas import tpu as pltpu
from jax.sharding import PartitionSpec as P

F32 = jnp.float32
BF16 = jnp.bfloat16
VMEM_LIMIT = 54 * 1024 * 1024
ROUTE_LIMIT = 54 * 1024 * 1024
TILE = 512
CHUNKS = 4
GATE = pl.CostEstimate(flops=1, bytes_accessed=1, transcendentals=0)
SMALL = pl.CostEstimate(flops=1, bytes_accessed=1, transcendentals=0)
TOKEN = jax.ShapeDtypeStruct((8, 128), F32)
ANY = pl.BlockSpec(memory_space=pl.ANY)


def route_kernel(plan, chosen, count, *refs):
    meta = refs[0]
    ins, refs = refs[chosen : chosen + count], refs[chosen + count :]
    outs, (_, sems) = refs[: len(plan)], refs[len(plan) :]
    moves = []
    for out, pieces in zip(outs, plan):
        for dst, rows, selector, options in pieces:
            step = rows // CHUNKS
            for c in range(CHUNKS):
                made = [
                    pltpu.make_async_copy(
                        ins[i].at[:, pl.ds(row + c * step, step), :],
                        out.at[:, pl.ds(dst + c * step, step), :],
                        sems.at[len(moves)],
                    )
                    for i, row in options
                ]
                moves.append((selector, made))
    for selector, made in moves:
        if selector is None:
            made[0].start()
        else:
            for value, copy in enumerate(made):
                pl.when(meta[selector] == value)(copy.start)
    for _, made in moves:
        made[0].wait()


def route(meta, outputs, after, in_vmem):
    arrays, place = [], {}
    plan = []
    for pieces in outputs:
        listed = []
        for dst, rows, selector, options in pieces:
            numbered = []
            for array, row in options:
                if id(array) not in place:
                    place[id(array)] = len(arrays)
                    arrays.append(array)
                numbered.append((place[id(array)], row))
            listed.append((dst, rows, selector, numbered))
        plan.append(listed)
    width = arrays[0].shape[2]
    heights = [sum(piece[1] for piece in pieces) for pieces in plan]
    arrays += after
    shape_of = pltpu.VMEM if in_vmem else jax.ShapeDtypeStruct
    chosen = any(piece[2] is not None for pieces in plan for piece in pieces)
    return pl.pallas_call(
        functools.partial(route_kernel, plan, int(chosen), len(arrays)),
        in_specs=[pl.BlockSpec(memory_space=pltpu.SMEM)] * chosen + [ANY] * len(arrays),
        out_specs=[pl.BlockSpec(memory_space=pltpu.VMEM)] * len(plan) + [ANY],
        out_shape=[shape_of((2, h, width), F32) for h in heights] + [TOKEN],
        scratch_shapes=[pltpu.SemaphoreType.DMA((CHUNKS * sum(len(p) for p in plan),))],
        compiler_params=pltpu.CompilerParams(vmem_limit_bytes=ROUTE_LIMIT),
        cost_estimate=GATE,
    )(*[meta] * chosen, *arrays)


def split(x):
    hi = x.astype(BF16)
    return hi, (x - hi.astype(F32)).astype(BF16)


def parts_of(re, im):
    out = []
    for x in (re, im, re + im):
        out.extend(split(x))
    return out


def split_kernel(block, ref, out, _, *left):
    parts = parts_of(ref[0], ref[1])
    for index, value in enumerate(parts):
        out[index] = value
    for left_out in left:
        for i in range(3):
            for c in range(ref.shape[2] // block):
                cols = slice(c * block, (c + 1) * block)
                for slot, value in enumerate((parts[2 * i], parts[2 * i], parts[2 * i + 1])):
                    left_out[i, :, pl.ds((3 * c + slot) * block, block)] = value[:, cols]


def split_block(x, block, with_left):
    _, rows, width = x.shape
    step = max(block, 256)
    out_specs = [pl.BlockSpec((6, rows, step), lambda n: (0, 0, n)), ANY]
    out_shape = [jax.ShapeDtypeStruct((6, rows, width), BF16), TOKEN]
    if with_left:
        out_specs.append(pl.BlockSpec((3, rows, 3 * step), lambda n: (0, 0, n)))
        out_shape.append(jax.ShapeDtypeStruct((3, rows, 3 * width), BF16))
    return pl.pallas_call(
        functools.partial(split_kernel, block),
        grid=(width // step,),
        in_specs=[pl.BlockSpec((2, rows, step), lambda n: (0, 0, n))],
        out_specs=out_specs,
        out_shape=out_shape,
        compiler_params=pltpu.CompilerParams(vmem_limit_bytes=VMEM_LIMIT),
        cost_estimate=SMALL,
    )(x)


def fetcher(places, sources, raw, sems, k, t):
    total = raw.shape[2]
    pieces = len(places[0])
    part = total // pieces
    cols = pl.ds(t * TILE, TILE)

    def spot(p):
        return raw.at[k, :, pl.ds(p * part, part), cols]

    def start(meta):
        for c in range(4):

            @pl.when(meta[k] == c)
            def _():
                for p, (index, row) in enumerate(places[c]):
                    source = sources[index].at[:, pl.ds(row, part), cols]
                    pltpu.make_async_copy(source, spot(p), sems.at[k, p, t]).start()

    def wait():
        for p in range(pieces):
            pltpu.make_async_copy(spot(p), spot(p), sems.at[k, p, t]).wait()

    return start, wait


def forward_kernel(pairs, places, count, has_sum, give_parts, partners, planes, shift, first, groups, meta, *refs):
    left_ref, refs = refs[0], refs[1:]
    sources, refs = refs[:count], refs[count:]
    if has_sum:
        f_in, refs = refs[0], refs[1:]
    p_refs, refs = refs[:partners], refs[partners:]
    f_out, _, refs = refs[0], refs[1], refs[2:]
    if give_parts:
        parts_out, refs = refs[0], refs[1:]
    if partners:
        tr_out, refs = refs[0], refs[1:]
    used = len(places)
    raws, raw_sems, refs = refs[:used], refs[used : 2 * used], refs[2 * used :]
    left, f_held, rights, sums, refs = refs[0], refs[1], refs[2:4], refs[4:6], refs[6:]
    sems, refs = refs[0], refs[1:]
    if give_parts:
        parts, refs = refs[0], refs[1:]
    if partners:
        p_held, refs = refs[0], refs[1:]
    total, width = raws[0].shape[2:]
    rows = f_held.shape[2]
    steps = [(t, k) for t in range(width // TILE) for k in range(pairs)]
    fetches = [
        [fetcher(places[g], sources, raws[g], raw_sems[g], k, t) for g in range(used)] for t, k in steps
    ]

    def tile_of(i):
        return pl.ds(steps[i][0] * TILE, TILE)

    def load_left(g):
        column = (lax.rem(meta[pairs] + shift, planes) * groups + first + g) * 3 * total
        cols = pl.ds(pl.multiple_of(column, 3 * total), 3 * total)
        return pltpu.make_async_copy(
            left_ref.at[:, :, cols], left.at[:, :, pl.ds(g * 3 * total, 3 * total)], sems.at[0, g]
        )

    def load_sum(i):
        spot = (steps[i][1], slice(None), slice(None), tile_of(i))
        return pltpu.make_async_copy(f_in.at[spot], f_held.at[spot], sems.at[1, i])

    def load_partners(i):
        copies, row = [], 0
        for index, p_ref in enumerate(p_refs):
            high = p_ref.shape[2]
            copies.append(
                pltpu.make_async_copy(
                    p_ref.at[steps[i][1], :, :, tile_of(i)],
                    p_held.at[steps[i][1], :, pl.ds(row, high), tile_of(i)],
                    sems.at[2 + index, i],
                )
            )
            row += high
        return copies

    def give_sum(i):
        spot = (steps[i][1], slice(None), slice(None), tile_of(i))
        return pltpu.make_async_copy(f_held.at[spot], f_out.at[spot], sems.at[4, i])

    def give_split(i):
        spot = (slice(None), pl.ds(steps[i][1] * total, total), tile_of(i))
        return pltpu.make_async_copy(parts.at[spot], parts_out.at[spot], sems.at[5, i])

    def split_step(i, which):
        t, k = steps[i]
        for g in range(used):
            re, im = raws[g][k, 0, :, tile_of(i)], raws[g][k, 1, :, tile_of(i)]
            high, low = split((re, im, re + im)[which])
            base = g * 3 * total
            for slot, value in enumerate((high, low, high)):
                rights[i % 2][which, pl.ds(base + slot * total, total), :] = value
            if give_parts:
                parts[2 * which, pl.ds(k * total, total), tile_of(i)] = high
                parts[2 * which + 1, pl.ds(k * total, total), tile_of(i)] = low

    def finish(i, half):
        k = steps[i][1]
        band = pl.ds(half * (rows // 2), rows // 2)
        t0, t1, t2 = (sums[i % 2][which, band, :] for which in range(3))
        fr, fi = t0 - t1, t2 - t0 - t1
        if has_sum:
            fr, fi = fr + f_held[k, 0, band, tile_of(i)], fi + f_held[k, 1, band, tile_of(i)]
        f_held[k, 0, band, tile_of(i)] = fr
        f_held[k, 1, band, tile_of(i)] = fi
        if partners:
            term = fr * p_held[k, 0, band, tile_of(i)] + fi * p_held[k, 1, band, tile_of(i)]
            term = jnp.sum(term.reshape(rows // 16, 8, TILE), axis=0)
            tr_out[k] += sum(term[:, c * 128 : (c + 1) * 128] for c in range(TILE // 128))

    if partners:
        tr_out[...] = jnp.zeros_like(tr_out)
    for i in range(len(steps)):
        for start, _ in fetches[i]:
            start(meta)
        if i == 0:
            for g in range(used):
                load_left(g).start()
        if i > 0 and has_sum:
            load_sum(i - 1).start()
        if i > 0:
            for copy in load_partners(i - 1):
                copy.start()
    if has_sum:
        load_sum(len(steps) - 1).start()
    for copy in load_partners(len(steps) - 1):
        copy.start()

    def arrive(i):
        if has_sum:
            load_sum(i).wait()
        for copy in load_partners(i):
            copy.wait()

    for _, wait in fetches[0]:
        wait()
    for which in range(3):
        split_step(0, which)
    for g in range(used):
        load_left(g).wait()
    for i in range(len(steps)):
        if i + 1 < len(steps):
            for _, wait in fetches[i + 1]:
                wait()
        if i > 0:
            arrive(i - 1)
        if give_parts:
            give_split(i).start()
        for which in range(3):
            sums[i % 2][which] = jnp.dot(left[which], rights[i % 2][which], preferred_element_type=F32)
            if i + 1 < len(steps):
                split_step(i + 1, which)
            if i > 0 and which < 2:
                finish(i - 1, which)
        if i > 0:
            give_sum(i - 1).start()
    last = len(steps) - 1
    arrive(last)
    finish(last, 0)
    finish(last, 1)
    give_sum(last).start()
    for i in range(len(steps)):
        give_sum(i).wait()
        if give_parts:
            give_split(i).wait()


def partner_kernel(planes, meta, x_ref, *refs):
    blocks, (p_out, _, x_held, b_held, p_held, *sums, x_sems, b_sems, out_sems) = refs[:planes], refs[planes:]
    pairs = p_out.shape[0]
    total = p_out.shape[2]
    rows = blocks[0].shape[1]
    tiles = b_held.shape[0]

    def load_x(i):
        two = pl.ds(2 * i, 2)
        return pltpu.make_async_copy(x_ref.at[two], x_held.at[two], x_sems.at[i])

    def load_b(i, j, t):
        two, cols = pl.ds(2 * i, 2), pl.ds(t * TILE, TILE)
        at = pl.multiple_of(lax.rem(meta[pairs] + j, planes) * rows, rows)
        return pltpu.make_async_copy(
            blocks[j].at[two, :, cols], b_held.at[t, two, pl.ds(at, rows), :], b_sems.at[i, j, t]
        )

    def give(t):
        spot = (slice(None), slice(None), slice(None), pl.ds(t * TILE, TILE))
        return pltpu.make_async_copy(p_held.at[spot], p_out.at[spot], out_sems.at[t])

    def finish(t, k):
        band = pl.ds(k * total, total)
        t0, t1, t2 = (sums[t % 2][i, band, :] for i in range(3))
        p_held[k, 0, :, pl.ds(t * TILE, TILE)] = t0 - t1
        p_held[k, 1, :, pl.ds(t * TILE, TILE)] = t2 - t0 - t1

    for t in range(tiles):
        for i in range(3):
            if t == 0:
                load_x(i).start()
            for j in range(planes):
                load_b(i, j, t).start()
    for t in range(tiles):
        for i in range(3):
            if t == 0:
                load_x(i).wait()
            for j in range(planes):
                load_b(i, j, t).wait()
            ah, al, bh, bl = x_held[2 * i], x_held[2 * i + 1], b_held[t, 2 * i], b_held[t, 2 * i + 1]
            term = jnp.dot(ah, bh, preferred_element_type=F32)
            term += jnp.dot(ah, bl, preferred_element_type=F32)
            sums[t % 2][i] = term + jnp.dot(al, bh, preferred_element_type=F32)
            if t > 0 and i < pairs:
                finish(t - 1, i)
        if t > 0:
            give(t - 1).start()
    for k in range(pairs):
        finish(tiles - 1, k)
    give(tiles - 1).start()
    for t in range(tiles):
        give(t).wait()


def placed(groups_of_cands):
    sources, places = [], []
    for cands in groups_of_cands:
        listed = []
        for pieces in cands:
            entry = []
            for array, row in pieces:
                known = [i for i, s in enumerate(sources) if s is array]
                if not known:
                    sources.append(array)
                entry.append((known[0] if known else len(sources) - 1, row))
            listed.append(entry)
        places.append(listed)
    return sources, places


def fetch_scratch(pairs, total, width, pieces):
    return pltpu.VMEM((pairs, 2, total, width), F32), pltpu.SemaphoreType.DMA((pairs, pieces, width // TILE))


def forward_call(meta, left, groups_of_cands, f, partners, shift, first, groups, give_parts):
    pairs = f_pairs(meta)
    _, rows, width = left.shape
    width //= 3
    planes = width // rows
    total = rows // groups
    sources, places = placed(groups_of_cands)
    used = len(places)
    steps = width // TILE * pairs
    out_specs = [ANY, ANY]
    out_shape = [jax.ShapeDtypeStruct((pairs, 2, rows, width), F32), TOKEN]
    scratch = [fetch_scratch(pairs, total, width, len(places[0][0])) for _ in places]
    scratch = [raw for raw, _ in scratch] + [sems for _, sems in scratch]
    scratch.append(pltpu.VMEM((3, rows, used * 3 * total), BF16))
    scratch.append(pltpu.VMEM((pairs, 2, rows, width), F32))
    scratch += [pltpu.VMEM((3, used * 3 * total, TILE), BF16)] * 2
    scratch += [pltpu.VMEM((3, rows, TILE), F32)] * 2
    scratch.append(pltpu.SemaphoreType.DMA((6, max(steps, used))))
    if give_parts:
        out_specs.append(ANY)
        out_shape.append(jax.ShapeDtypeStruct((6, pairs * total, width), BF16))
        scratch.append(pltpu.VMEM((6, pairs * total, width), BF16))
    if partners:
        out_specs.append(pl.BlockSpec(memory_space=pltpu.VMEM))
        out_shape.append(jax.ShapeDtypeStruct((pairs, 8, 128), F32))
        scratch.append(pltpu.VMEM((pairs, 2, rows, width), F32))
    args = [meta, left, *sources]
    aliases = {}
    if f is not None:
        aliases = {len(args): 0}
        args.append(f)
    args += partners
    return pl.pallas_call(
        functools.partial(
            forward_kernel,
            pairs,
            places,
            len(sources),
            f is not None,
            give_parts,
            len(partners),
            planes,
            shift,
            first,
            groups,
        ),
        in_specs=[pl.BlockSpec(memory_space=pltpu.SMEM)] + [ANY] * (len(args) - 1),
        out_specs=out_specs,
        out_shape=out_shape,
        scratch_shapes=scratch,
        input_output_aliases=aliases,
        compiler_params=pltpu.CompilerParams(vmem_limit_bytes=VMEM_LIMIT),
        cost_estimate=SMALL,
    )(*args)


def partner_call(meta, x6, blocks6):
    pairs = f_pairs(meta)
    planes = len(blocks6)
    _, rows, width = blocks6[0].shape
    total = x6.shape[1] // pairs
    tiles = width // TILE
    return pl.pallas_call(
        functools.partial(partner_kernel, planes),
        in_specs=[pl.BlockSpec(memory_space=pltpu.SMEM)] + [ANY] * (1 + planes),
        out_specs=[ANY, ANY],
        out_shape=[jax.ShapeDtypeStruct((pairs, 2, total, width), F32), TOKEN],
        scratch_shapes=[
            pltpu.VMEM((6, pairs * total, width), BF16),
            pltpu.VMEM((tiles, 6, width, TILE), BF16),
            pltpu.VMEM((pairs, 2, total, width), F32),
            pltpu.VMEM((3, pairs * total, TILE), F32),
            pltpu.VMEM((3, pairs * total, TILE), F32),
            pltpu.SemaphoreType.DMA((3,)),
            pltpu.SemaphoreType.DMA((3, planes, tiles)),
            pltpu.SemaphoreType.DMA((tiles,)),
        ],
        compiler_params=pltpu.CompilerParams(vmem_limit_bytes=VMEM_LIMIT),
        cost_estimate=SMALL,
    )(meta, x6, *blocks6)


def f_pairs(meta):
    return meta.shape[0] - 3


STEPS = {
    2: (
        ([("z", 0, 0)], [], []),
        ([("z", 0, 1)], [], []),
        ([("x", 0, 0), ("z", 0, 2)], [("own", 0)], []),
        ([("x", 0, 1), ("z", 0, 3)], [], []),
        ([("x", 0, 2)], [], []),
        ([("x", 0, 3), ("z", 1, 0), ("z", 1, 2), ("zy", 1, 1), ("c", 0, 0)], [("other", 0)], [("x", 0, 2)]),
        ([("x", 1, 0), ("z", 1, 3), ("xy", 1, 1), ("c", 0, 1)], [("forward", 0)], [("z", 1, 1)]),
        ([("x", 1, 2), ("xy", 1, 3), ("c", 1, 0)], [("partner", 0), ("forward", 1)], []),
        ([("c", 1, 1)], [("partner", 1)], []),
    ),
    1: (
        ([("z", 0, 0)], [], []),
        ([("z", 0, 1)], [], []),
        ([("x", 0, 0)], [("own", 0)], []),
        ([("x", 0, 1), ("z", 1, 0), ("zy", 1, 1)], [], []),
        ([("x", 1, 0), ("c", 0, 0), ("xy", 1, 1)], [("other", 0)], []),
        ([("c", 1, 0)], [("forward", 0), ("partner", 0)], []),
    ),
}


def body(fields, offsets):
    own = fields[0]
    pairs = offsets.shape[1]
    _, rows, width = own.shape
    steps = lax.axis_size("tm")
    planes = lax.axis_size("mode")
    me = lax.axis_index("tm")
    lane = lax.rem(me, 2)
    odd_chip = lax.rem(lax.div(me, 2), 2)
    groups = 2 if rows >= 512 else 1
    part = rows // groups // 2

    distance = offsets[0]
    place = jnp.where((lane == 1) & (distance % 2 == 1), 3 - distance, distance - 1)
    meta = jnp.concatenate([place, jnp.stack([lax.axis_index("mode"), odd_chip, lane])]).astype(jnp.int32)
    odd_at, lane_at = pairs + 1, pairs + 2

    def from_later(x):
        return lax.ppermute(x, "tm", [((i + 4) % steps, i) for i in range(steps)])

    def from_plane(x, shift):
        return lax.ppermute(x, "mode", [((i + shift) % planes, i) for i in range(planes)])

    def across_chips(x):
        return lax.ppermute(x, "tm", [(i ^ 2, i) for i in range(steps)])

    def across_cores(x):
        return lax.ppermute(x, "tm", [(i ^ 1, i) for i in range(steps)])

    got = {}

    def here(j, q):
        if j == 0:
            return own, q * part
        return got["y", j], q * part

    def operand(kind, j, q):
        if kind == "z":
            return [(0, part, None, [here(j, q)])]
        if kind in ("zy", "xy"):
            return [(0, part, None, [(got[kind[0], 0, q], 0)])]
        if kind == "x":
            return [(0, part, odd_at, [(got["z", j, q], 0), here(j, q)])]
        pieces = (2 * q, 2 * q + 1)
        out = [(i * part, part, None, [(got["x", j, p], 0)]) for i, p in enumerate(pieces)]
        return out + [
            ((i + 2) * part, part, lane_at, [(got["z", j, p], 0), here(j, p)]) for i, p in enumerate(pieces)
        ]

    def send(kind, j, q, x):
        if kind in ("zy", "xy"):
            return from_plane(x, j)
        if kind == "z":
            return from_later(x)
        if kind == "x":
            return across_chips(x)
        return across_cores(x)

    def candidates(j, group):
        picks = (2 * group, 2 * group + 1)
        swapped = got["c", j, group]
        return [
            [(swapped, 2 * part), (swapped, 3 * part)],
            [(got["x", j, q], 0) for q in picks],
            [(swapped, 0), (swapped, part)],
            [(got["z", j, q], 0) for q in picks],
        ]

    f, own6, left, others6, parts6, partners = None, None, None, {}, {}, []

    for j in range(1, planes):
        got["y", j] = from_plane(own, j)
    written = []
    for step, work, there in STEPS[groups]:
        tasks, after = [], list(written[-1:])
        for kind, other, q in step:
            tasks += [(kind, j, q) for j in (range(1, planes) if other else [0])]
        after += [got[kind, j, q] for kind, other, q in there for j in (range(1, planes) if other else [0])]
        for kind, g in work:
            if kind == "own":
                own6, done, left = split_block(own, 2 * part, True)
                after.append(done)
            elif kind == "other":
                for j in range(1, planes):
                    others6[j], done = split_block(got["y", j], 2 * part, False)
                    after.append(done)
            elif kind == "forward":
                f, done, parts6[g] = forward_call(meta, left, [candidates(0, g)], f, [], 0, g, groups, True)
                after.append(done)
            else:
                blocks6 = [own6] + [others6[i] for i in range(1, planes)]
                partner, done = partner_call(meta, parts6[g], blocks6)
                partners.append(partner)
                after.append(done)
        written = route(meta, [operand(*task) for task in tasks], after, planes == 2)
        for (kind, j, q), x in zip(tasks, written[:-1]):
            got[kind[0], j, q] = send(kind, j, q, x)

    for j in range(1, planes):
        last = j == planes - 1
        cands = [candidates(j, g) for g in range(groups)]
        out = forward_call(meta, left, cands, f, partners if last else [], j, 0, groups, False)
        f = out[0]
    partial_trace = jnp.sum(out[2], axis=(1, 2)) / F32(width)
    if planes == 2:
        traces = partial_trace + from_plane(partial_trace, 1)
    else:
        traces = lax.psum(partial_trace, "mode")
    return (f[None], traces[None])


def solution(mesh):
    in_specs = (P("tm", None, "mode", None), P("tm", None))
    out_specs = (P("tm", None, None, "mode", None), P("tm", None))
    return jax.shard_map(body, mesh=mesh, in_specs=in_specs, out_specs=out_specs, check_vma=False)
```

```python
import functools

import jax
import jax.numpy as jnp
from jax import lax
from jax.experimental import pallas as pl
from jax.experimental.pallas import tpu as pltpu
from jax.sharding import PartitionSpec as P

F32 = jnp.float32
BF16 = jnp.bfloat16
VMEM_LIMIT = 54 * 1024 * 1024
ROUTE_LIMIT = 54 * 1024 * 1024
TILE = 512
SPLIT_TILE = 256
CHUNKS = 4
GATE = pl.CostEstimate(flops=1, bytes_accessed=1, transcendentals=0)
SMALL = pl.CostEstimate(flops=1, bytes_accessed=1, transcendentals=0)
TOKEN = jax.ShapeDtypeStruct((8, 128), F32)
ANY = pl.BlockSpec(memory_space=pl.ANY)
IN_VMEM = pl.BlockSpec(memory_space=pltpu.VMEM)


def held(x):
    return pltpu.with_memory_space_constraint(x, pltpu.VMEM)


def route_kernel(plan, chosen, count, *refs):
    meta = refs[0]
    ins, refs = refs[chosen : chosen + count], refs[chosen + count :]
    outs, (_, sems) = refs[: len(plan)], refs[len(plan) :]
    moves = []
    for out, pieces in zip(outs, plan):
        for dst, rows, selector, options in pieces:
            step = rows // CHUNKS
            for c in range(CHUNKS):
                made = [
                    pltpu.make_async_copy(
                        ins[i].at[:, pl.ds(row + c * step, step), :],
                        out.at[:, pl.ds(dst + c * step, step), :],
                        sems.at[len(moves)],
                    )
                    for i, row in options
                ]
                moves.append((selector, made))
    for selector, made in moves:
        if selector is None:
            made[0].start()
        else:
            for value, copy in enumerate(made):
                pl.when(meta[selector] == value)(copy.start)
    for _, made in moves:
        made[0].wait()


def route(meta, outputs, after, in_vmem):
    arrays, place = [], {}
    plan = []
    for pieces in outputs:
        listed = []
        for dst, rows, selector, options in pieces:
            numbered = []
            for array, row in options:
                if id(array) not in place:
                    place[id(array)] = len(arrays)
                    arrays.append(array)
                numbered.append((place[id(array)], row))
            listed.append((dst, rows, selector, numbered))
        plan.append(listed)
    width = arrays[0].shape[2]
    heights = [sum(piece[1] for piece in pieces) for pieces in plan]
    arrays += after
    shape_of = pltpu.VMEM if in_vmem else jax.ShapeDtypeStruct
    chosen = any(piece[2] is not None for pieces in plan for piece in pieces)
    return pl.pallas_call(
        functools.partial(route_kernel, plan, int(chosen), len(arrays)),
        in_specs=[pl.BlockSpec(memory_space=pltpu.SMEM)] * chosen + [ANY] * len(arrays),
        out_specs=[pl.BlockSpec(memory_space=pltpu.VMEM)] * len(plan) + [ANY],
        out_shape=[shape_of((2, h, width), F32) for h in heights] + [TOKEN],
        scratch_shapes=[pltpu.SemaphoreType.DMA((CHUNKS * sum(len(p) for p in plan),))],
        compiler_params=pltpu.CompilerParams(vmem_limit_bytes=ROUTE_LIMIT),
        cost_estimate=GATE,
    )(*[meta] * chosen, *arrays)


def split(x):
    hi = x.astype(BF16)
    return hi, (x - hi.astype(F32)).astype(BF16)


def parts_of(re, im):
    out = []
    for x in (re, im, re + im):
        out.extend(split(x))
    return out


def split_kernel(x_ref, out, _):
    for index, value in enumerate(parts_of(x_ref[0], x_ref[1])):
        out[index] = value


def split_block(x):
    _, rows, width = x.shape
    return pl.pallas_call(
        split_kernel,
        grid=(width // SPLIT_TILE,),
        in_specs=[pl.BlockSpec((2, rows, SPLIT_TILE), lambda n: (0, 0, n))],
        out_specs=[pl.BlockSpec((6, rows, SPLIT_TILE), lambda n: (0, 0, n)), ANY],
        out_shape=[jax.ShapeDtypeStruct((6, rows, width), BF16), TOKEN],
        compiler_params=pltpu.CompilerParams(vmem_limit_bytes=VMEM_LIMIT),
        cost_estimate=SMALL,
    )(x)


def fetch_start(meta, places, sources, raw, sems, k, t):
    part = raw.shape[2] // len(places[0])
    cols = pl.ds(t * TILE, TILE)
    for c in range(4):

        @pl.when(meta[k] == c)
        def _():
            for p, (index, row) in enumerate(places[c]):
                source = sources[index].at[:, pl.ds(row, part), cols]
                spot = raw.at[k, :, pl.ds(p * part, part), cols]
                pltpu.make_async_copy(source, spot, sems.at[k, p, t]).start()


def fetch_wait(places, raw, sems, k, t, cols):
    part = raw.shape[2] // len(places[0])
    for p in range(len(places[0])):
        spot = raw.at[k, :, pl.ds(p * part, part), cols]
        pltpu.make_async_copy(spot, spot, sems.at[k, p, t]).wait()


def tile_at(t):
    return pl.ds(pl.multiple_of(t * TILE, TILE), TILE)


def own_columns(own6, left6, sem, block, total):
    cols = pl.ds(pl.multiple_of(block * total, total), total)
    return pltpu.make_async_copy(own6.at[:, :, cols], left6, sem.at[0])


def lay_left(left6, left):
    total = left6.shape[2]
    for which in range(3):
        for slot, index in enumerate((2 * which, 2 * which, 2 * which + 1)):
            left[which, :, pl.ds(slot * total, total)] = left6[index]


def lay_right(right, which, high, low):
    total = high.shape[0]
    for slot, value in enumerate((high, low, high)):
        right[which, pl.ds(slot * total, total), :] = value


def products(left, right, sums):
    rows = left.shape[1]
    for which in range(3):
        sums[which, pl.ds(0, rows), :] = jnp.dot(left[which], right[which], preferred_element_type=F32)


def both_kernel(places, count, has_sum, planes, group, groups, meta, own6, *refs):
    sources, refs = refs[:count], refs[count:]
    blocks, refs = (own6, *refs[: planes - 1]), refs[planes - 1 :]
    if has_sum:
        f_in, refs = refs[0], refs[1:]
    f_out, p_out, _, raw, left6, left, *refs = refs
    (rights, sums), (parts, held, f_held, p_held, *sems) = (refs[:2], refs[2:4]), refs[4:]
    raw_sems, left_sem, block_sems, in_sems, out_sems, p_sems = sems
    pairs, _, total, width = raw.shape
    rows = left.shape[1]
    tiles = width // TILE
    plane = meta[pairs]

    def load_sum(t, k):
        spot = (k, slice(None), slice(None), tile_at(t))
        return pltpu.make_async_copy(f_in.at[spot], f_held.at[spot], in_sems.at[t, k])

    def give_sum(t, k):
        spot = (k, slice(None), slice(None), tile_at(t))
        return pltpu.make_async_copy(f_held.at[spot], f_out.at[spot], out_sems.at[t, k])

    def load_block(j, t):
        return pltpu.make_async_copy(blocks[j].at[:, :, tile_at(t)], held.at[j, :, :, tile_at(t)], block_sems.at[j, t])

    def give_partner(t):
        spot = (slice(None), slice(None), slice(None), tile_at(t))
        return pltpu.make_async_copy(p_held.at[spot], p_out.at[spot], p_sems.at[t])

    load_left = own_columns(own6, left6, left_sem, plane * groups + group, total)
    load_left.start()
    for t in range(tiles):
        for k in range(pairs):
            fetch_start(meta, places, sources, raw, raw_sems, k, t)
            if has_sum:
                load_sum(t, k).start()
    for t in range(tiles):
        for j in range(planes):
            load_block(j, t).start()
    load_left.wait()
    lay_left(left6, left)

    def lay(t, k):
        cols, band = tile_at(t), pl.ds(k * total, total)
        fetch_wait(places, raw, raw_sems, k, t, cols)
        re, im = raw[k, 0, :, cols], raw[k, 1, :, cols]
        for which, value in enumerate((re, im, re + im)):
            high, low = split(value)
            lay_right(rights[k % 2], which, high, low)
            parts[2 * which, band, cols] = high
            parts[2 * which + 1, band, cols] = low

    def finish(t, k):
        cols = tile_at(t)
        t0, t1, t2 = (sums[k % 2][which, pl.ds(0, rows), :] for which in range(3))
        fr, fi = t0 - t1, t2 - t0 - t1
        if has_sum:
            fr, fi = fr + f_held[k, 0, :, cols], fi + f_held[k, 1, :, cols]
        f_held[k, 0, :, cols] = fr
        f_held[k, 1, :, cols] = fi

    def forward(t, carry):
        if has_sum:
            for k in range(pairs):
                load_sum(t, k).wait()
        lay(t, 0)
        for k in range(pairs):
            if k + 1 < pairs:
                lay(t, k + 1)
            products(left, rights[k % 2], sums[k % 2])
            if k > 0:
                finish(t, k - 1)
        finish(t, pairs - 1)
        for k in range(pairs):
            give_sum(t, k).start()
        return carry

    lax.fori_loop(0, tiles, forward, 0)

    def partner(t, carry):
        cols = tile_at(t)
        for j in range(planes):
            load_block(j, t).wait()

        for i in range(3):
            term = None
            for j in range(planes):
                at = pl.multiple_of(lax.rem(plane + j, planes) * rows, rows)
                ah, al = parts[2 * i, :, pl.ds(at, rows)], parts[2 * i + 1, :, pl.ds(at, rows)]
                bh, bl = held[j, 2 * i, :, cols], held[j, 2 * i + 1, :, cols]
                for a, b in ((ah, bh), (ah, bl), (al, bh)):
                    more = jnp.dot(a, b, preferred_element_type=F32)
                    term = more if term is None else term + more
            sums[0][i, pl.ds(0, pairs * total), :] = term
        for k in range(pairs):
            t0, t1, t2 = (sums[0][i, pl.ds(k * total, total), :] for i in range(3))
            p_held[k, 0, :, cols] = t0 - t1
            p_held[k, 1, :, cols] = t2 - t0 - t1
        give_partner(t).start()
        return carry

    lax.fori_loop(0, tiles, partner, 0)
    for t in range(tiles):
        for k in range(pairs):
            give_sum(t, k).wait()
        give_partner(t).wait()


def more_kernel(places, count, partners, planes, shift, group, groups, meta, own6, *refs):
    sources, refs = refs[:count], refs[count:]
    f_in, refs = refs[0], refs[1:]
    p_refs, refs = refs[:partners], refs[partners:]
    f_out, refs = refs[0], refs[1:]
    if partners:
        tr_out, refs = refs[0], refs[1:]
    raw, left6, left, *refs = refs
    (rights, sums), (f_held, raw_sems, left_sem, sems, *p_held) = (refs[:2], refs[2:4]), refs[4:]
    pairs, _, total, width = raw.shape
    rows = left.shape[1]
    tiles = width // TILE

    def load_sum(t, k):
        spot = (k, slice(None), slice(None), tile_at(t))
        return pltpu.make_async_copy(f_in.at[spot], f_held.at[spot], sems.at[0, t, k])

    def give_sum(t, k):
        spot = (k, slice(None), slice(None), tile_at(t))
        return pltpu.make_async_copy(f_held.at[spot], f_out.at[spot], sems.at[1, t, k])

    def load_partners(t, k):
        copies, row = [], 0
        for index, p_ref in enumerate(p_refs):
            high = p_ref.shape[2]
            there = p_held[0].at[k, :, pl.ds(row, high), tile_at(t)]
            copies.append(pltpu.make_async_copy(p_ref.at[k, :, :, tile_at(t)], there, sems.at[2 + index, t, k]))
            row += high
        return copies

    load_left = own_columns(own6, left6, left_sem, lax.rem(meta[pairs] + shift, planes) * groups + group, total)
    load_left.start()
    for t in range(tiles):
        for k in range(pairs):
            fetch_start(meta, places, sources, raw, raw_sems, k, t)
            load_sum(t, k).start()
            for copy in load_partners(t, k):
                copy.start()
    if partners:
        tr_out[...] = jnp.zeros_like(tr_out)
    load_left.wait()
    lay_left(left6, left)

    def lay(t, k):
        cols = tile_at(t)
        fetch_wait(places, raw, raw_sems, k, t, cols)
        re, im = raw[k, 0, :, cols], raw[k, 1, :, cols]
        for which, value in enumerate((re, im, re + im)):
            lay_right(rights[k % 2], which, *split(value))

    def finish(t, k):
        cols = tile_at(t)
        t0, t1, t2 = (sums[k % 2][which, pl.ds(0, rows), :] for which in range(3))
        fr, fi = t0 - t1 + f_held[k, 0, :, cols], t2 - t0 - t1 + f_held[k, 1, :, cols]
        f_held[k, 0, :, cols] = fr
        f_held[k, 1, :, cols] = fi
        if partners:
            term = fr * p_held[0][k, 0, :, cols] + fi * p_held[0][k, 1, :, cols]
            term = jnp.sum(term.reshape(rows // 8, 8, TILE), axis=0)
            tr_out[k] += sum(term[:, c * 128 : (c + 1) * 128] for c in range(TILE // 128))

    def forward(t, carry):
        lay(t, 0)
        for k in range(pairs):
            load_sum(t, k).wait()
            for copy in load_partners(t, k):
                copy.wait()
            if k + 1 < pairs:
                lay(t, k + 1)
            products(left, rights[k % 2], sums[k % 2])
            if k > 0:
                finish(t, k - 1)
        finish(t, pairs - 1)
        for k in range(pairs):
            give_sum(t, k).start()
        return carry

    lax.fori_loop(0, tiles, forward, 0)
    for t in range(tiles):
        for k in range(pairs):
            give_sum(t, k).wait()


def placed(groups_of_cands):
    sources, places = [], []
    for cands in groups_of_cands:
        listed = []
        for pieces in cands:
            entry = []
            for array, row in pieces:
                known = [i for i, s in enumerate(sources) if s is array]
                if not known:
                    sources.append(array)
                entry.append((known[0] if known else len(sources) - 1, row))
            listed.append(entry)
        places.append(listed)
    return sources, places


def fetch_scratch(pairs, total, width, pieces):
    return pltpu.VMEM((pairs, 2, total, width), F32), pltpu.SemaphoreType.DMA((pairs, pieces, width // TILE))


def operand_scratch(rows, total, high):
    return [
        pltpu.VMEM((6, rows, total), BF16),
        pltpu.VMEM((3, rows, 3 * total), BF16),
        *[pltpu.VMEM((3, 3 * total, TILE), BF16)] * 2,
        *[pltpu.VMEM((3, high, TILE), F32)] * 2,
    ]


def both_call(meta, own6, others6, cands, f, group, groups):
    pairs = f_pairs(meta)
    planes = 1 + len(others6)
    _, rows, width = own6.shape
    total = rows // groups
    tiles = width // TILE
    sources, (places,) = placed([cands])
    raw, raw_sems = fetch_scratch(pairs, total, width, len(places[0]))
    args = [meta, own6, *sources, *others6]
    aliases = {}
    if f is not None:
        aliases = {len(args): 0}
        args.append(f)
    return pl.pallas_call(
        functools.partial(both_kernel, places, len(sources), f is not None, planes, group, groups),
        in_specs=[pl.BlockSpec(memory_space=pltpu.SMEM)] + [ANY] * (len(args) - 1),
        out_specs=[ANY] * 3,
        out_shape=[
            jax.ShapeDtypeStruct((pairs, 2, rows, width), F32),
            jax.ShapeDtypeStruct((pairs, 2, total, width), F32),
            TOKEN,
        ],
        scratch_shapes=[
            raw,
            *operand_scratch(rows, total, max(rows, pairs * total)),
            pltpu.VMEM((6, pairs * total, width), BF16),
            pltpu.VMEM((planes, 6, rows, width), BF16),
            pltpu.VMEM((pairs, 2, rows, width), F32),
            pltpu.VMEM((pairs, 2, total, width), F32),
            raw_sems,
            pltpu.SemaphoreType.DMA((1,)),
            pltpu.SemaphoreType.DMA((planes, tiles)),
            pltpu.SemaphoreType.DMA((tiles, pairs)),
            pltpu.SemaphoreType.DMA((tiles, pairs)),
            pltpu.SemaphoreType.DMA((tiles,)),
        ],
        input_output_aliases=aliases,
        compiler_params=pltpu.CompilerParams(vmem_limit_bytes=VMEM_LIMIT),
        cost_estimate=SMALL,
    )(*args)


def more_call(meta, own6, cands, f, partners, shift, group, groups):
    pairs = f_pairs(meta)
    _, rows, width = own6.shape
    planes = width // rows
    total = rows // groups
    tiles = width // TILE
    sources, (places,) = placed([cands])
    raw, raw_sems = fetch_scratch(pairs, total, width, len(places[0]))
    out_specs = [ANY]
    out_shape = [jax.ShapeDtypeStruct((pairs, 2, rows, width), F32)]
    scratch = [raw, *operand_scratch(rows, total, rows), pltpu.VMEM((pairs, 2, rows, width), F32), raw_sems]
    scratch += [pltpu.SemaphoreType.DMA((1,)), pltpu.SemaphoreType.DMA((2 + len(partners), tiles, pairs))]
    if partners:
        out_specs.append(IN_VMEM)
        out_shape.append(jax.ShapeDtypeStruct((pairs, 8, 128), F32))
        scratch.append(pltpu.VMEM((pairs, 2, rows, width), F32))
    args = [meta, own6, *sources, f, *partners]
    return pl.pallas_call(
        functools.partial(more_kernel, places, len(sources), len(partners), planes, shift, group, groups),
        in_specs=[pl.BlockSpec(memory_space=pltpu.SMEM)] + [ANY] * (len(args) - 1),
        out_specs=out_specs,
        out_shape=out_shape,
        scratch_shapes=scratch,
        input_output_aliases={2 + len(sources): 0},
        compiler_params=pltpu.CompilerParams(vmem_limit_bytes=VMEM_LIMIT),
        cost_estimate=SMALL,
    )(*args)


def f_pairs(meta):
    return meta.shape[0] - 3


STEPS = {
    2: (
        ([("z", 0, 0)], [], []),
        ([("z", 0, 1)], [], []),
        ([("x", 0, 0), ("z", 0, 2)], [("own", 0)], []),
        ([("x", 0, 1), ("z", 0, 3)], [], []),
        ([("x", 0, 2)], [], []),
        ([("x", 0, 3), ("z", 1, 0), ("z", 1, 2), ("zy", 1, 1), ("c", 0, 0)], [("other", 0)], [("x", 0, 2)]),
        ([("x", 1, 0), ("z", 1, 3), ("xy", 1, 1), ("c", 0, 1)], [], [("z", 1, 1)]),
        ([("x", 1, 2), ("xy", 1, 3), ("c", 1, 0)], [("both", 0)], []),
        ([("c", 1, 1)], [("both", 1)], []),
    ),
    1: (
        ([("z", 0, 0)], [], []),
        ([("z", 0, 1)], [], []),
        ([("x", 0, 0)], [("own", 0)], []),
        ([("x", 0, 1), ("z", 1, 0), ("zy", 1, 1)], [], []),
        ([("x", 1, 0), ("c", 0, 0), ("xy", 1, 1)], [("other", 0)], []),
        ([("c", 1, 0)], [("both", 0)], []),
    ),
}


def body(fields, offsets):
    own = fields[0]
    pairs = offsets.shape[1]
    _, rows, width = own.shape
    steps = lax.axis_size("tm")
    planes = lax.axis_size("mode")
    me = lax.axis_index("tm")
    lane = lax.rem(me, 2)
    odd_chip = lax.rem(lax.div(me, 2), 2)
    groups = 2 if rows >= 512 else 1
    part = rows // groups // 2

    distance = offsets[0]
    place = jnp.where((lane == 1) & (distance % 2 == 1), 3 - distance, distance - 1)
    meta = jnp.concatenate([place, jnp.stack([lax.axis_index("mode"), odd_chip, lane])]).astype(jnp.int32)
    odd_at, lane_at = pairs + 1, pairs + 2

    def from_later(x):
        return lax.ppermute(x, "tm", [((i + 4) % steps, i) for i in range(steps)])

    def from_plane(x, shift):
        return lax.ppermute(x, "mode", [((i + shift) % planes, i) for i in range(planes)])

    def across_chips(x):
        return lax.ppermute(x, "tm", [(i ^ 2, i) for i in range(steps)])

    def across_cores(x):
        return lax.ppermute(x, "tm", [(i ^ 1, i) for i in range(steps)])

    got = {}

    def here(j, q):
        if j == 0:
            return own, q * part
        return got["y", j], q * part

    def operand(kind, j, q):
        if kind == "z":
            return [(0, part, None, [here(j, q)])]
        if kind in ("zy", "xy"):
            return [(0, part, None, [(got[kind[0], 0, q], 0)])]
        if kind == "x":
            arrived = held(got["z", j, q]) if planes == 2 else got["z", j, q]
            return [(0, part, odd_at, [(arrived, 0), here(j, q)])]
        pieces = (2 * q, 2 * q + 1)
        out = [(i * part, part, None, [(got["x", j, p], 0)]) for i, p in enumerate(pieces)]
        return out + [
            ((i + 2) * part, part, lane_at, [(got["z", j, p], 0), here(j, p)]) for i, p in enumerate(pieces)
        ]

    def send(kind, j, q, x):
        if kind in ("zy", "xy"):
            return from_plane(x, j)
        if kind == "z":
            return from_later(x)
        if kind == "x":
            return across_chips(x)
        return across_cores(x)

    def candidates(j, group, near=False):
        picks = (2 * group, 2 * group + 1)
        swapped = held(got["c", j, group]) if near else got["c", j, group]
        cross4 = [(swapped, 2 * part), (swapped, 3 * part)]
        cross2 = [(swapped, 0), (swapped, part)]
        return [
            cross4,
            [(got["x", j, q], 0) for q in picks],
            cross2,
            [(got["z", j, q], 0) for q in picks],
        ]

    f, own6, others6, partners = None, None, [], []

    for j in range(1, planes):
        got["y", j] = from_plane(own, j)
    written = []
    for step, work, there in STEPS[groups]:
        tasks, after = [], list(written[-1:])
        for kind, other, q in step:
            tasks += [(kind, j, q) for j in (range(1, planes) if other else [0])]
        after += [got[kind, j, q] for kind, other, q in there for j in (range(1, planes) if other else [0])]
        for kind, g in work:
            if kind == "own":
                own6, done = split_block(own)
                after.append(done)
            elif kind == "other":
                for j in range(1, planes):
                    block6, done = split_block(got["y", j])
                    others6.append(block6)
                    after.append(done)
            else:
                f, partner, done = both_call(meta, own6, others6, candidates(0, g), f, g, groups)
                partners.append(partner)
                after.append(done)
        written = route(meta, [operand(*task) for task in tasks], after, planes == 2)
        for (kind, j, q), x in zip(tasks, written[:-1]):
            got[kind[0], j, q] = send(kind, j, q, x)

    for g in range(groups):
        for j in range(1, planes):
            last = g == groups - 1 and j == planes - 1
            out = more_call(meta, own6, candidates(j, g, last and planes == 2), f, partners if last else [], j, g, groups)
            f = out[0]
    partial_trace = jnp.sum(out[1], axis=(1, 2)) / F32(width)
    if planes == 2:
        traces = partial_trace + from_plane(partial_trace, 1)
    else:
        traces = lax.psum(partial_trace, "mode")
    return (f[None], traces[None])


def solution(mesh):
    in_specs = (P("tm", None, "mode", None), P("tm", None))
    out_specs = (P("tm", None, None, "mode", None), P("tm", None))
    return jax.shard_map(body, mesh=mesh, in_specs=in_specs, out_specs=out_specs, check_vma=False)
```

```python
import functools

import jax
import jax.numpy as jnp
from jax import lax
from jax.experimental import pallas as pl
from jax.experimental.pallas import tpu as pltpu
from jax.sharding import PartitionSpec as P

F32 = jnp.float32
BF16 = jnp.bfloat16
VMEM_LIMIT = 54 * 1024 * 1024
ROUTE_LIMIT = 54 * 1024 * 1024
TILE = 512
SPLIT_TILE = 256
CHUNKS = 4
GATE = pl.CostEstimate(flops=1, bytes_accessed=1, transcendentals=0)
SMALL = pl.CostEstimate(flops=1, bytes_accessed=1, transcendentals=0)
TOKEN = jax.ShapeDtypeStruct((8, 128), F32)
ANY = pl.BlockSpec(memory_space=pl.ANY)
IN_VMEM = pl.BlockSpec(memory_space=pltpu.VMEM)


def held(x):
    return pltpu.with_memory_space_constraint(x, pltpu.VMEM)


def route_kernel(plan, chosen, count, *refs):
    meta = refs[0]
    ins, refs = refs[chosen : chosen + count], refs[chosen + count :]
    outs, (_, sems) = refs[: len(plan)], refs[len(plan) :]
    moves = []
    for out, pieces in zip(outs, plan):
        for dst, rows, selector, options in pieces:
            step = rows // CHUNKS
            for c in range(CHUNKS):
                made = [
                    pltpu.make_async_copy(
                        ins[i].at[:, pl.ds(row + c * step, step), :],
                        out.at[:, pl.ds(dst + c * step, step), :],
                        sems.at[len(moves)],
                    )
                    for i, row in options
                ]
                moves.append((selector, made))
    for selector, made in moves:
        if selector is None:
            made[0].start()
        else:
            for value, copy in enumerate(made):
                pl.when(meta[selector] == value)(copy.start)
    for _, made in moves:
        made[0].wait()


def route(meta, outputs, after, near):
    arrays, place = [], {}
    plan = []
    for pieces in outputs:
        listed = []
        for dst, rows, selector, options in pieces:
            numbered = []
            for array, row in options:
                if id(array) not in place:
                    place[id(array)] = len(arrays)
                    arrays.append(array)
                numbered.append((place[id(array)], row))
            listed.append((dst, rows, selector, numbered))
        plan.append(listed)
    width = arrays[0].shape[2]
    heights = [sum(piece[1] for piece in pieces) for pieces in plan]
    arrays += after
    chosen = any(piece[2] is not None for pieces in plan for piece in pieces)
    return pl.pallas_call(
        functools.partial(route_kernel, plan, int(chosen), len(arrays)),
        in_specs=[pl.BlockSpec(memory_space=pltpu.SMEM)] * chosen + [ANY] * len(arrays),
        out_specs=[pl.BlockSpec(memory_space=pltpu.VMEM)] * len(plan) + [ANY],
        out_shape=[
            (pltpu.VMEM if n else jax.ShapeDtypeStruct)((2, h, width), F32) for n, h in zip(near, heights)
        ]
        + [TOKEN],
        scratch_shapes=[pltpu.SemaphoreType.DMA((CHUNKS * sum(len(p) for p in plan),))],
        compiler_params=pltpu.CompilerParams(vmem_limit_bytes=ROUTE_LIMIT),
        cost_estimate=GATE,
    )(*[meta] * chosen, *arrays)


def split(x):
    hi = x.astype(BF16)
    return hi, (x - hi.astype(F32)).astype(BF16)


def parts_of(re, im):
    out = []
    for x in (re, im, re + im):
        out.extend(split(x))
    return out


def split_kernel(x_ref, out, _):
    for index, value in enumerate(parts_of(x_ref[0], x_ref[1])):
        out[index] = value


def split_block(x):
    _, rows, width = x.shape
    return pl.pallas_call(
        split_kernel,
        grid=(width // SPLIT_TILE,),
        in_specs=[pl.BlockSpec((2, rows, SPLIT_TILE), lambda n: (0, 0, n))],
        out_specs=[pl.BlockSpec((6, rows, SPLIT_TILE), lambda n: (0, 0, n)), ANY],
        out_shape=[jax.ShapeDtypeStruct((6, rows, width), BF16), TOKEN],
        compiler_params=pltpu.CompilerParams(vmem_limit_bytes=VMEM_LIMIT),
        cost_estimate=SMALL,
    )(x)


def fetch_start(meta, places, sources, raw, sems, k, t):
    part = raw.shape[2] // len(places[0])
    cols = pl.ds(t * TILE, TILE)
    for c in range(4):

        @pl.when(meta[k] == c)
        def _():
            for p, (index, row) in enumerate(places[c]):
                source = sources[index].at[:, pl.ds(row, part), cols]
                spot = raw.at[k, :, pl.ds(p * part, part), cols]
                pltpu.make_async_copy(source, spot, sems.at[k, p, t]).start()


def fetch_wait(places, raw, sems, k, t, cols):
    part = raw.shape[2] // len(places[0])
    for p in range(len(places[0])):
        spot = raw.at[k, :, pl.ds(p * part, part), cols]
        pltpu.make_async_copy(spot, spot, sems.at[k, p, t]).wait()


def tile_at(t):
    return pl.ds(pl.multiple_of(t * TILE, TILE), TILE)


def own_columns(own6, left6, sem, block, total):
    cols = pl.ds(pl.multiple_of(block * total, total), total)
    return pltpu.make_async_copy(own6.at[:, :, cols], left6, sem.at[0])


def lay_left(left6, left):
    total = left6.shape[2]
    for which in range(3):
        for slot, index in enumerate((2 * which, 2 * which, 2 * which + 1)):
            left[which, :, pl.ds(slot * total, total)] = left6[index]


def lay_right(right, which, high, low):
    total = high.shape[0]
    for slot, value in enumerate((high, low, high)):
        right[which, pl.ds(slot * total, total), :] = value


def products(left, right, sums):
    rows = left.shape[1]
    for which in range(3):
        sums[which, pl.ds(0, rows), :] = jnp.dot(left[which], right[which], preferred_element_type=F32)


def both_kernel(places, count, has_sum, planes, group, groups, meta, own6, *refs):
    sources, refs = refs[:count], refs[count:]
    blocks, refs = (own6, *refs[: planes - 1]), refs[planes - 1 :]
    if has_sum:
        f_in, refs = refs[0], refs[1:]
    f_out, p_out, _, raw, left6, left, *refs = refs
    (rights, sums), (parts, held, f_held, p_held, *sems) = (refs[:2], refs[2:4]), refs[4:]
    raw_sems, left_sem, block_sems, in_sems, out_sems, p_sems = sems
    pairs, _, total, width = raw.shape
    rows = left.shape[1]
    tiles = width // TILE
    plane = meta[pairs]

    def load_sum(t, k):
        spot = (k, slice(None), slice(None), tile_at(t))
        return pltpu.make_async_copy(f_in.at[spot], f_held.at[spot], in_sems.at[t, k])

    def give_sum(t, k):
        spot = (k, slice(None), slice(None), tile_at(t))
        return pltpu.make_async_copy(f_held.at[spot], f_out.at[spot], out_sems.at[t, k])

    def load_block(j, t):
        return pltpu.make_async_copy(blocks[j].at[:, :, tile_at(t)], held.at[j, :, :, tile_at(t)], block_sems.at[j, t])

    def give_partner(t):
        spot = (slice(None), slice(None), slice(None), tile_at(t))
        return pltpu.make_async_copy(p_held.at[spot], p_out.at[spot], p_sems.at[t])

    load_left = own_columns(own6, left6, left_sem, plane * groups + group, total)
    load_left.start()
    for t in range(tiles):
        for k in range(pairs):
            fetch_start(meta, places, sources, raw, raw_sems, k, t)
            if has_sum:
                load_sum(t, k).start()
    for t in range(tiles):
        for j in range(planes):
            load_block(j, t).start()
    load_left.wait()
    lay_left(left6, left)

    def lay(t, k):
        cols, band = tile_at(t), pl.ds(k * total, total)
        fetch_wait(places, raw, raw_sems, k, t, cols)
        re, im = raw[k, 0, :, cols], raw[k, 1, :, cols]
        for which, value in enumerate((re, im, re + im)):
            high, low = split(value)
            lay_right(rights[k % 2], which, high, low)
            parts[2 * which, band, cols] = high
            parts[2 * which + 1, band, cols] = low

    def finish(t, k):
        cols = tile_at(t)
        t0, t1, t2 = (sums[k % 2][which, pl.ds(0, rows), :] for which in range(3))
        fr, fi = t0 - t1, t2 - t0 - t1
        if has_sum:
            fr, fi = fr + f_held[k, 0, :, cols], fi + f_held[k, 1, :, cols]
        f_held[k, 0, :, cols] = fr
        f_held[k, 1, :, cols] = fi

    def forward(t, carry):
        if has_sum:
            for k in range(pairs):
                load_sum(t, k).wait()
        lay(t, 0)
        for k in range(pairs):
            if k + 1 < pairs:
                lay(t, k + 1)
            products(left, rights[k % 2], sums[k % 2])
            if k > 0:
                finish(t, k - 1)
        finish(t, pairs - 1)
        for k in range(pairs):
            give_sum(t, k).start()
        return carry

    lax.fori_loop(0, tiles, forward, 0)

    def partner(t, carry):
        cols = tile_at(t)
        for j in range(planes):
            load_block(j, t).wait()

        for i in range(3):
            term = None
            for j in range(planes):
                at = pl.multiple_of(lax.rem(plane + j, planes) * rows, rows)
                ah, al = parts[2 * i, :, pl.ds(at, rows)], parts[2 * i + 1, :, pl.ds(at, rows)]
                bh, bl = held[j, 2 * i, :, cols], held[j, 2 * i + 1, :, cols]
                for a, b in ((ah, bh), (ah, bl), (al, bh)):
                    more = jnp.dot(a, b, preferred_element_type=F32)
                    term = more if term is None else term + more
            sums[0][i, pl.ds(0, pairs * total), :] = term
        for k in range(pairs):
            t0, t1, t2 = (sums[0][i, pl.ds(k * total, total), :] for i in range(3))
            p_held[k, 0, :, cols] = t0 - t1
            p_held[k, 1, :, cols] = t2 - t0 - t1
        give_partner(t).start()
        return carry

    lax.fori_loop(0, tiles, partner, 0)
    for t in range(tiles):
        for k in range(pairs):
            give_sum(t, k).wait()
        give_partner(t).wait()


def more_kernel(places, count, partners, planes, shift, group, groups, meta, own6, *refs):
    sources, refs = refs[:count], refs[count:]
    f_in, refs = refs[0], refs[1:]
    p_refs, refs = refs[:partners], refs[partners:]
    f_out, _, refs = refs[0], refs[1], refs[2:]
    if partners:
        tr_out, refs = refs[0], refs[1:]
    raw, left6, left, *refs = refs
    (rights, sums), (f_held, raw_sems, left_sem, sems, *p_held) = (refs[:2], refs[2:4]), refs[4:]
    pairs, _, total, width = raw.shape
    rows = left.shape[1]
    tiles = width // TILE

    def load_sum(t, k):
        spot = (k, slice(None), slice(None), tile_at(t))
        return pltpu.make_async_copy(f_in.at[spot], f_held.at[spot], sems.at[0, t, k])

    def give_sum(t, k):
        spot = (k, slice(None), slice(None), tile_at(t))
        return pltpu.make_async_copy(f_held.at[spot], f_out.at[spot], sems.at[1, t, k])

    def load_partners(t, k):
        copies, row = [], 0
        for index, p_ref in enumerate(p_refs):
            high = p_ref.shape[2]
            there = p_held[0].at[k, :, pl.ds(row, high), tile_at(t)]
            copies.append(pltpu.make_async_copy(p_ref.at[k, :, :, tile_at(t)], there, sems.at[2 + index, t, k]))
            row += high
        return copies

    load_left = own_columns(own6, left6, left_sem, lax.rem(meta[pairs] + shift, planes) * groups + group, total)
    load_left.start()
    for t in range(tiles):
        for k in range(pairs):
            fetch_start(meta, places, sources, raw, raw_sems, k, t)
            load_sum(t, k).start()
            for copy in load_partners(t, k):
                copy.start()
    if partners:
        tr_out[...] = jnp.zeros_like(tr_out)
    load_left.wait()
    lay_left(left6, left)

    def lay(t, k):
        cols = tile_at(t)
        fetch_wait(places, raw, raw_sems, k, t, cols)
        re, im = raw[k, 0, :, cols], raw[k, 1, :, cols]
        for which, value in enumerate((re, im, re + im)):
            lay_right(rights[k % 2], which, *split(value))

    def finish(t, k):
        cols = tile_at(t)
        t0, t1, t2 = (sums[k % 2][which, pl.ds(0, rows), :] for which in range(3))
        fr, fi = t0 - t1 + f_held[k, 0, :, cols], t2 - t0 - t1 + f_held[k, 1, :, cols]
        f_held[k, 0, :, cols] = fr
        f_held[k, 1, :, cols] = fi
        if partners:
            term = fr * p_held[0][k, 0, :, cols] + fi * p_held[0][k, 1, :, cols]
            term = jnp.sum(term.reshape(rows // 8, 8, TILE), axis=0)
            tr_out[k] += sum(term[:, c * 128 : (c + 1) * 128] for c in range(TILE // 128))

    def forward(t, carry):
        lay(t, 0)
        for k in range(pairs):
            load_sum(t, k).wait()
            for copy in load_partners(t, k):
                copy.wait()
            if k + 1 < pairs:
                lay(t, k + 1)
            products(left, rights[k % 2], sums[k % 2])
            if k > 0:
                finish(t, k - 1)
        finish(t, pairs - 1)
        for k in range(pairs):
            give_sum(t, k).start()
        return carry

    lax.fori_loop(0, tiles, forward, 0)
    for t in range(tiles):
        for k in range(pairs):
            give_sum(t, k).wait()


def placed(groups_of_cands):
    sources, places = [], []
    for cands in groups_of_cands:
        listed = []
        for pieces in cands:
            entry = []
            for array, row in pieces:
                known = [i for i, s in enumerate(sources) if s is array]
                if not known:
                    sources.append(array)
                entry.append((known[0] if known else len(sources) - 1, row))
            listed.append(entry)
        places.append(listed)
    return sources, places


def fetch_scratch(pairs, total, width, pieces):
    return pltpu.VMEM((pairs, 2, total, width), F32), pltpu.SemaphoreType.DMA((pairs, pieces, width // TILE))


def operand_scratch(rows, total, high):
    return [
        pltpu.VMEM((6, rows, total), BF16),
        pltpu.VMEM((3, rows, 3 * total), BF16),
        *[pltpu.VMEM((3, 3 * total, TILE), BF16)] * 2,
        *[pltpu.VMEM((3, high, TILE), F32)] * 2,
    ]


def both_call(meta, own6, others6, cands, f, group, groups):
    pairs = f_pairs(meta)
    planes = 1 + len(others6)
    _, rows, width = own6.shape
    total = rows // groups
    tiles = width // TILE
    sources, (places,) = placed([cands])
    raw, raw_sems = fetch_scratch(pairs, total, width, len(places[0]))
    args = [meta, own6, *sources, *others6]
    aliases = {}
    if f is not None:
        aliases = {len(args): 0}
        args.append(f)
    return pl.pallas_call(
        functools.partial(both_kernel, places, len(sources), f is not None, planes, group, groups),
        in_specs=[pl.BlockSpec(memory_space=pltpu.SMEM)] + [ANY] * (len(args) - 1),
        out_specs=[ANY] * 3,
        out_shape=[
            jax.ShapeDtypeStruct((pairs, 2, rows, width), F32),
            jax.ShapeDtypeStruct((pairs, 2, total, width), F32),
            TOKEN,
        ],
        scratch_shapes=[
            raw,
            *operand_scratch(rows, total, max(rows, pairs * total)),
            pltpu.VMEM((6, pairs * total, width), BF16),
            pltpu.VMEM((planes, 6, rows, width), BF16),
            pltpu.VMEM((pairs, 2, rows, width), F32),
            pltpu.VMEM((pairs, 2, total, width), F32),
            raw_sems,
            pltpu.SemaphoreType.DMA((1,)),
            pltpu.SemaphoreType.DMA((planes, tiles)),
            pltpu.SemaphoreType.DMA((tiles, pairs)),
            pltpu.SemaphoreType.DMA((tiles, pairs)),
            pltpu.SemaphoreType.DMA((tiles,)),
        ],
        input_output_aliases=aliases,
        compiler_params=pltpu.CompilerParams(vmem_limit_bytes=VMEM_LIMIT),
        cost_estimate=SMALL,
    )(*args)


def more_call(meta, own6, cands, f, partners, shift, group, groups):
    pairs = f_pairs(meta)
    _, rows, width = own6.shape
    planes = width // rows
    total = rows // groups
    tiles = width // TILE
    sources, (places,) = placed([cands])
    raw, raw_sems = fetch_scratch(pairs, total, width, len(places[0]))
    out_specs = [ANY, ANY]
    out_shape = [jax.ShapeDtypeStruct((pairs, 2, rows, width), F32), TOKEN]
    scratch = [raw, *operand_scratch(rows, total, rows), pltpu.VMEM((pairs, 2, rows, width), F32), raw_sems]
    scratch += [pltpu.SemaphoreType.DMA((1,)), pltpu.SemaphoreType.DMA((2 + len(partners), tiles, pairs))]
    if partners:
        out_specs.append(IN_VMEM)
        out_shape.append(jax.ShapeDtypeStruct((pairs, 8, 128), F32))
        scratch.append(pltpu.VMEM((pairs, 2, rows, width), F32))
    args = [meta, own6, *sources, f, *partners]
    return pl.pallas_call(
        functools.partial(more_kernel, places, len(sources), len(partners), planes, shift, group, groups),
        in_specs=[pl.BlockSpec(memory_space=pltpu.SMEM)] + [ANY] * (len(args) - 1),
        out_specs=out_specs,
        out_shape=out_shape,
        scratch_shapes=scratch,
        input_output_aliases={2 + len(sources): 0},
        compiler_params=pltpu.CompilerParams(vmem_limit_bytes=VMEM_LIMIT),
        cost_estimate=SMALL,
    )(*args)


def f_pairs(meta):
    return meta.shape[0] - 3


STEPS = {
    2: (
        ([("z", 0, 0)], [], []),
        ([("z", 0, 1)], [], []),
        ([("x", 0, 0), ("z", 0, 2)], [("own", 0)], []),
        ([("x", 0, 1), ("z", 0, 3)], [], []),
        ([("x", 0, 2)], [], []),
        ([("x", 0, 3), ("z", 1, 0), ("z", 1, 2), ("zy", 1, 1), ("c", 0, 0), ("d", 0, 1)], [("other", 0)], []),
        ([("x", 1, 0), ("z", 1, 3), ("xy", 1, 1), ("xy", 1, 3), ("e", 0, 3)], [("both", 0)], [("z", 1, 1)]),
        ([("x", 1, 2), ("c", 1, 0)], [("both", 1)], []),
        ([("c", 1, 1)], [("more", 0)], []),
    ),
    1: (
        ([("z", 0, 0)], [], []),
        ([("z", 0, 1)], [], []),
        ([("x", 0, 0)], [("own", 0)], []),
        ([("x", 0, 1), ("z", 1, 0), ("zy", 1, 1)], [], []),
        ([("x", 1, 0), ("c", 0, 0), ("xy", 1, 1)], [("other", 0)], []),
        ([("c", 1, 0)], [("both", 0)], []),
    ),
}


def body(fields, offsets):
    own = fields[0]
    pairs = offsets.shape[1]
    _, rows, width = own.shape
    steps = lax.axis_size("tm")
    planes = lax.axis_size("mode")
    me = lax.axis_index("tm")
    lane = lax.rem(me, 2)
    odd_chip = lax.rem(lax.div(me, 2), 2)
    groups = 2 if rows >= 512 else 1
    part = rows // groups // 2

    distance = offsets[0]
    place = jnp.where((lane == 1) & (distance % 2 == 1), 3 - distance, distance - 1)
    meta = jnp.concatenate([place, jnp.stack([lax.axis_index("mode"), odd_chip, lane])]).astype(jnp.int32)
    odd_at, lane_at = pairs + 1, pairs + 2

    def from_later(x):
        return lax.ppermute(x, "tm", [((i + 4) % steps, i) for i in range(steps)])

    def from_plane(x, shift):
        return lax.ppermute(x, "mode", [((i + shift) % planes, i) for i in range(planes)])

    def across_chips(x):
        return lax.ppermute(x, "tm", [(i ^ 2, i) for i in range(steps)])

    def across_cores(x):
        return lax.ppermute(x, "tm", [(i ^ 1, i) for i in range(steps)])

    got = {}

    def here(j, q):
        if j == 0:
            return own, q * part
        return got["y", j], q * part

    def operand(kind, j, q):
        if kind == "z":
            return [(0, part, None, [here(j, q)])]
        if kind in ("zy", "xy", "e"):
            return [(0, part, None, [(got["x" if kind == "e" else kind[0], 0, q], 0)])]
        if kind == "x":
            arrived = held(got["z", j, q]) if planes == 2 else got["z", j, q]
            return [(0, part, odd_at, [(arrived, 0), here(j, q)])]
        pieces = (2 * q, 2 * q + 1)
        pieces_x = pieces[:1] if kind == "d" else pieces
        out = [(i * part, part, None, [(got["x", j, p], 0)]) for i, p in enumerate(pieces_x)]
        return out + [
            ((i + len(pieces_x)) * part, part, lane_at, [(got["z", j, p], 0), here(j, p)]) for i, p in enumerate(pieces)
        ]

    def send(kind, j, q, x):
        if kind in ("zy", "xy"):
            return from_plane(x, j)
        if kind == "z":
            return from_later(x)
        if kind == "x":
            return across_chips(x)
        return across_cores(x)

    def candidates(j, group, near=False):
        picks = (2 * group, 2 * group + 1)
        if ("c", j, group) in got:
            swapped = held(got["c", j, group]) if near else got["c", j, group]
            cross4 = [(swapped, 2 * part), (swapped, 3 * part)]
            cross2 = [(swapped, 0), (swapped, part)]
        else:
            swapped = got["d", j, group]
            cross4 = [(swapped, part), (swapped, 2 * part)]
            cross2 = [(swapped, 0), (got["e", j, picks[1]], 0)]
        return [
            cross4,
            [(got["x", j, q], 0) for q in picks],
            cross2,
            [(got["z", j, q], 0) for q in picks],
        ]

    f, own6, others6, partners = None, None, [], []

    for j in range(1, planes):
        got["y", j] = from_plane(own, j)
    written = []
    for step, work, there in STEPS[groups]:
        tasks, after = [], list(written[-1:])
        for kind, other, q in step:
            tasks += [(kind, j, q) for j in (range(1, planes) if other else [0])]
        after += [got[kind, j, q] for kind, other, q in there for j in (range(1, planes) if other else [0])]
        for kind, g in work:
            if kind == "own":
                own6, done = split_block(own)
                after.append(done)
            elif kind == "other":
                for j in range(1, planes):
                    block6, done = split_block(got["y", j])
                    others6.append(block6)
                    after.append(done)
            elif kind == "more":
                for j in range(1, planes):
                    f, done = more_call(meta, own6, candidates(j, g), f, [], j, g, groups)
                    after.append(done)
            else:
                f, partner, done = both_call(meta, own6, others6, candidates(0, g), f, g, groups)
                partners.append(partner)
                after.append(done)
        written = route(
            meta, [operand(*task) for task in tasks], after, [planes == 2 and task[0] != "d" for task in tasks]
        )
        for (kind, j, q), x in zip(tasks, written[:-1]):
            got[kind[0], j, q] = send(kind, j, q, x)

    for j in range(1, planes):
        near, last = planes == 2, j == planes - 1
        cands = candidates(j, groups - 1, near)
        out = more_call(meta, own6, cands, f, partners if last else [], j, groups - 1, groups)
        f = out[0]
    partial_trace = jnp.sum(out[2], axis=(1, 2)) / F32(width)
    if planes == 2:
        traces = partial_trace + from_plane(partial_trace, 1)
    else:
        traces = lax.psum(partial_trace, "mode")
    return (f[None], traces[None])


def solution(mesh):
    in_specs = (P("tm", None, "mode", None), P("tm", None))
    out_specs = (P("tm", None, None, "mode", None), P("tm", None))
    return jax.shard_map(body, mesh=mesh, in_specs=in_specs, out_specs=out_specs, check_vma=False)
```

```python
import functools

import jax
import jax.numpy as jnp
from jax import lax
from jax.experimental import pallas as pl
from jax.experimental.pallas import tpu as pltpu
from jax.sharding import PartitionSpec as P

F32 = jnp.float32
BF16 = jnp.bfloat16
VMEM_LIMIT = 54 * 1024 * 1024
ROUTE_LIMIT = 54 * 1024 * 1024
TILE = 512
SPLIT_TILE = 256
CHUNKS = 4
GATE = pl.CostEstimate(flops=1, bytes_accessed=1, transcendentals=0)
SMALL = pl.CostEstimate(flops=1, bytes_accessed=1, transcendentals=0)
TOKEN = jax.ShapeDtypeStruct((8, 128), F32)
ANY = pl.BlockSpec(memory_space=pl.ANY)
IN_VMEM = pl.BlockSpec(memory_space=pltpu.VMEM)


def held(x):
    return pltpu.with_memory_space_constraint(x, pltpu.VMEM)


def route_kernel(plan, chosen, count, *refs):
    meta = refs[0]
    ins, refs = refs[chosen : chosen + count], refs[chosen + count :]
    outs, (_, sems) = refs[: len(plan)], refs[len(plan) :]
    moves = []
    for out, pieces in zip(outs, plan):
        for dst, rows, selector, options in pieces:
            step = rows // CHUNKS
            for c in range(CHUNKS):
                made = [
                    pltpu.make_async_copy(
                        ins[i].at[:, pl.ds(row + c * step, step), :],
                        out.at[:, pl.ds(dst + c * step, step), :],
                        sems.at[len(moves)],
                    )
                    for i, row in options
                ]
                moves.append((selector, made))
    for selector, made in moves:
        if selector is None:
            made[0].start()
        else:
            for value, copy in enumerate(made):
                pl.when(meta[selector] == value)(copy.start)
    for _, made in moves:
        made[0].wait()


def route(meta, outputs, after, near):
    arrays, place = [], {}
    plan = []
    for pieces in outputs:
        listed = []
        for dst, rows, selector, options in pieces:
            numbered = []
            for array, row in options:
                if id(array) not in place:
                    place[id(array)] = len(arrays)
                    arrays.append(array)
                numbered.append((place[id(array)], row))
            listed.append((dst, rows, selector, numbered))
        plan.append(listed)
    width = arrays[0].shape[2]
    heights = [sum(piece[1] for piece in pieces) for pieces in plan]
    arrays += after
    chosen = any(piece[2] is not None for pieces in plan for piece in pieces)
    return pl.pallas_call(
        functools.partial(route_kernel, plan, int(chosen), len(arrays)),
        in_specs=[pl.BlockSpec(memory_space=pltpu.SMEM)] * chosen + [ANY] * len(arrays),
        out_specs=[pl.BlockSpec(memory_space=pltpu.VMEM)] * len(plan) + [ANY],
        out_shape=[
            (pltpu.VMEM if n else jax.ShapeDtypeStruct)((2, h, width), F32) for n, h in zip(near, heights)
        ]
        + [TOKEN],
        scratch_shapes=[pltpu.SemaphoreType.DMA((CHUNKS * sum(len(p) for p in plan),))],
        compiler_params=pltpu.CompilerParams(vmem_limit_bytes=ROUTE_LIMIT),
        cost_estimate=GATE,
    )(*[meta] * chosen, *arrays)


def split(x):
    hi = x.astype(BF16)
    return hi, (x - hi.astype(F32)).astype(BF16)


def parts_of(re, im):
    out = []
    for x in (re, im, re + im):
        out.extend(split(x))
    return out


def split_kernel(x_ref, out, _):
    for index, value in enumerate(parts_of(x_ref[0], x_ref[1])):
        out[index] = value


def split_block(x):
    _, rows, width = x.shape
    return pl.pallas_call(
        split_kernel,
        grid=(width // SPLIT_TILE,),
        in_specs=[pl.BlockSpec((2, rows, SPLIT_TILE), lambda n: (0, 0, n))],
        out_specs=[pl.BlockSpec((6, rows, SPLIT_TILE), lambda n: (0, 0, n)), ANY],
        out_shape=[jax.ShapeDtypeStruct((6, rows, width), BF16), TOKEN],
        compiler_params=pltpu.CompilerParams(vmem_limit_bytes=VMEM_LIMIT),
        cost_estimate=SMALL,
    )(x)


def fetch_start(meta, places, sources, raw, sems, k, t):
    part = raw.shape[2] // len(places[0])
    cols = pl.ds(t * TILE, TILE)
    for c in range(4):

        @pl.when(meta[k] == c)
        def _():
            for p, (index, row) in enumerate(places[c]):
                source = sources[index].at[:, pl.ds(row, part), cols]
                spot = raw.at[k, :, pl.ds(p * part, part), cols]
                pltpu.make_async_copy(source, spot, sems.at[k, p, t]).start()


def fetch_wait(places, raw, sems, k, t, cols):
    part = raw.shape[2] // len(places[0])
    for p in range(len(places[0])):
        spot = raw.at[k, :, pl.ds(p * part, part), cols]
        pltpu.make_async_copy(spot, spot, sems.at[k, p, t]).wait()


def tile_at(t):
    return pl.ds(pl.multiple_of(t * TILE, TILE), TILE)


def own_columns(own6, left6, sem, block, total):
    cols = pl.ds(pl.multiple_of(block * total, total), total)
    return pltpu.make_async_copy(own6.at[:, :, cols], left6, sem.at[0])


def lay_left(left6, left):
    total = left6.shape[2]
    for which in range(3):
        for slot, index in enumerate((2 * which, 2 * which, 2 * which + 1)):
            left[which, :, pl.ds(slot * total, total)] = left6[index]


def lay_right(right, which, high, low):
    total = high.shape[0]
    for slot, value in enumerate((high, low, high)):
        right[which, pl.ds(slot * total, total), :] = value


def products(left, right, sums):
    rows = left.shape[1]
    for which in range(3):
        sums[which, pl.ds(0, rows), :] = jnp.dot(left[which], right[which], preferred_element_type=F32)


def both_kernel(places, count, has_sum, planes, group, groups, meta, own6, *refs):
    sources, refs = refs[:count], refs[count:]
    blocks, refs = (own6, *refs[: planes - 1]), refs[planes - 1 :]
    if has_sum:
        f_in, refs = refs[0], refs[1:]
    f_out, p_out, _, raw, left6, left, *refs = refs
    (rights, sums), (parts, held, f_held, p_held, *sems) = (refs[:2], refs[2:4]), refs[4:]
    raw_sems, left_sem, block_sems, in_sems, out_sems, p_sems = sems
    pairs, _, total, width = raw.shape
    rows = left.shape[1]
    tiles = width // TILE
    plane = meta[pairs]

    def load_sum(t, k):
        spot = (k, slice(None), slice(None), tile_at(t))
        return pltpu.make_async_copy(f_in.at[spot], f_held.at[spot], in_sems.at[t, k])

    def give_sum(t, k):
        spot = (k, slice(None), slice(None), tile_at(t))
        return pltpu.make_async_copy(f_held.at[spot], f_out.at[spot], out_sems.at[t, k])

    def load_block(j, t):
        return pltpu.make_async_copy(blocks[j].at[:, :, tile_at(t)], held.at[j, :, :, tile_at(t)], block_sems.at[j, t])

    def give_partner(t):
        spot = (slice(None), slice(None), slice(None), tile_at(t))
        return pltpu.make_async_copy(p_held.at[spot], p_out.at[spot], p_sems.at[t])

    load_left = own_columns(own6, left6, left_sem, plane * groups + group, total)
    load_left.start()
    for t in range(tiles):
        for k in range(pairs):
            fetch_start(meta, places, sources, raw, raw_sems, k, t)
            if has_sum:
                load_sum(t, k).start()
    for t in range(tiles):
        for j in range(planes):
            load_block(j, t).start()
    load_left.wait()
    lay_left(left6, left)

    def lay(t, k):
        cols, band = tile_at(t), pl.ds(k * total, total)
        fetch_wait(places, raw, raw_sems, k, t, cols)
        re, im = raw[k, 0, :, cols], raw[k, 1, :, cols]
        for which, value in enumerate((re, im, re + im)):
            high, low = split(value)
            lay_right(rights[k % 2], which, high, low)
            parts[2 * which, band, cols] = high
            parts[2 * which + 1, band, cols] = low

    def finish(t, k):
        cols = tile_at(t)
        t0, t1, t2 = (sums[k % 2][which, pl.ds(0, rows), :] for which in range(3))
        fr, fi = t0 - t1, t2 - t0 - t1
        if has_sum:
            fr, fi = fr + f_held[k, 0, :, cols], fi + f_held[k, 1, :, cols]
        f_held[k, 0, :, cols] = fr
        f_held[k, 1, :, cols] = fi

    def forward(t, carry):
        if has_sum:
            for k in range(pairs):
                load_sum(t, k).wait()
        lay(t, 0)
        for k in range(pairs):
            if k + 1 < pairs:
                lay(t, k + 1)
            products(left, rights[k % 2], sums[k % 2])
            if k > 0:
                finish(t, k - 1)
        finish(t, pairs - 1)
        for k in range(pairs):
            give_sum(t, k).start()
        return carry

    lax.fori_loop(0, tiles, forward, 0)

    def partner(t, carry):
        cols = tile_at(t)
        for j in range(planes):
            load_block(j, t).wait()

        for i in range(3):
            term = None
            for j in range(planes):
                at = pl.multiple_of(lax.rem(plane + j, planes) * rows, rows)
                ah, al = parts[2 * i, :, pl.ds(at, rows)], parts[2 * i + 1, :, pl.ds(at, rows)]
                bh, bl = held[j, 2 * i, :, cols], held[j, 2 * i + 1, :, cols]
                for a, b in ((ah, bh), (ah, bl), (al, bh)):
                    more = jnp.dot(a, b, preferred_element_type=F32)
                    term = more if term is None else term + more
            sums[0][i, pl.ds(0, pairs * total), :] = term
        for k in range(pairs):
            t0, t1, t2 = (sums[0][i, pl.ds(k * total, total), :] for i in range(3))
            p_held[k, 0, :, cols] = t0 - t1
            p_held[k, 1, :, cols] = t2 - t0 - t1
        give_partner(t).start()
        return carry

    lax.fori_loop(0, tiles, partner, 0)
    for t in range(tiles):
        for k in range(pairs):
            give_sum(t, k).wait()
        give_partner(t).wait()


def more_kernel(places, count, partners, planes, shift, group, groups, meta, own6, *refs):
    sources, refs = refs[:count], refs[count:]
    f_in, refs = refs[0], refs[1:]
    p_refs, refs = refs[:partners], refs[partners:]
    f_out, _, refs = refs[0], refs[1], refs[2:]
    if partners:
        tr_out, refs = refs[0], refs[1:]
    raw, left6, left, *refs = refs
    (rights, sums), (f_held, raw_sems, left_sem, sems, *p_held) = (refs[:2], refs[2:4]), refs[4:]
    pairs, _, total, width = raw.shape
    rows = left.shape[1]
    tiles = width // TILE

    def load_sum(t, k):
        spot = (k, slice(None), slice(None), tile_at(t))
        return pltpu.make_async_copy(f_in.at[spot], f_held.at[spot], sems.at[0, t, k])

    def give_sum(t, k):
        spot = (k, slice(None), slice(None), tile_at(t))
        return pltpu.make_async_copy(f_held.at[spot], f_out.at[spot], sems.at[1, t, k])

    def load_partners(t, k):
        copies, row = [], 0
        for index, p_ref in enumerate(p_refs):
            high = p_ref.shape[2]
            there = p_held[0].at[k, :, pl.ds(row, high), tile_at(t)]
            copies.append(pltpu.make_async_copy(p_ref.at[k, :, :, tile_at(t)], there, sems.at[2 + index, t, k]))
            row += high
        return copies

    load_left = own_columns(own6, left6, left_sem, lax.rem(meta[pairs] + shift, planes) * groups + group, total)
    load_left.start()
    for t in range(tiles):
        for k in range(pairs):
            fetch_start(meta, places, sources, raw, raw_sems, k, t)
            load_sum(t, k).start()
            for copy in load_partners(t, k):
                copy.start()
    if partners:
        tr_out[...] = jnp.zeros_like(tr_out)
    load_left.wait()
    lay_left(left6, left)

    def lay(t, k):
        cols = tile_at(t)
        fetch_wait(places, raw, raw_sems, k, t, cols)
        re, im = raw[k, 0, :, cols], raw[k, 1, :, cols]
        for which, value in enumerate((re, im, re + im)):
            lay_right(rights[k % 2], which, *split(value))

    def finish(t, k):
        cols = tile_at(t)
        t0, t1, t2 = (sums[k % 2][which, pl.ds(0, rows), :] for which in range(3))
        fr, fi = t0 - t1 + f_held[k, 0, :, cols], t2 - t0 - t1 + f_held[k, 1, :, cols]
        f_held[k, 0, :, cols] = fr
        f_held[k, 1, :, cols] = fi
        if partners:
            term = fr * p_held[0][k, 0, :, cols] + fi * p_held[0][k, 1, :, cols]
            term = jnp.sum(term.reshape(rows // 8, 8, TILE), axis=0)
            tr_out[k] += sum(term[:, c * 128 : (c + 1) * 128] for c in range(TILE // 128))

    def forward(t, carry):
        lay(t, 0)
        for k in range(pairs):
            load_sum(t, k).wait()
            for copy in load_partners(t, k):
                copy.wait()
            if k + 1 < pairs:
                lay(t, k + 1)
            products(left, rights[k % 2], sums[k % 2])
            if k > 0:
                finish(t, k - 1)
        finish(t, pairs - 1)
        for k in range(pairs):
            give_sum(t, k).start()
        return carry

    lax.fori_loop(0, tiles, forward, 0)
    for t in range(tiles):
        for k in range(pairs):
            give_sum(t, k).wait()


def placed(groups_of_cands):
    sources, places = [], []
    for cands in groups_of_cands:
        listed = []
        for pieces in cands:
            entry = []
            for array, row in pieces:
                known = [i for i, s in enumerate(sources) if s is array]
                if not known:
                    sources.append(array)
                entry.append((known[0] if known else len(sources) - 1, row))
            listed.append(entry)
        places.append(listed)
    return sources, places


def fetch_scratch(pairs, total, width, pieces):
    return pltpu.VMEM((pairs, 2, total, width), F32), pltpu.SemaphoreType.DMA((pairs, pieces, width // TILE))


def operand_scratch(rows, total, high):
    return [
        pltpu.VMEM((6, rows, total), BF16),
        pltpu.VMEM((3, rows, 3 * total), BF16),
        *[pltpu.VMEM((3, 3 * total, TILE), BF16)] * 2,
        *[pltpu.VMEM((3, high, TILE), F32)] * 2,
    ]


def both_call(meta, own6, others6, cands, f, group, groups):
    pairs = f_pairs(meta)
    planes = 1 + len(others6)
    _, rows, width = own6.shape
    total = rows // groups
    tiles = width // TILE
    sources, (places,) = placed([cands])
    raw, raw_sems = fetch_scratch(pairs, total, width, len(places[0]))
    args = [meta, own6, *sources, *others6]
    aliases = {}
    if f is not None:
        aliases = {len(args): 0}
        args.append(f)
    return pl.pallas_call(
        functools.partial(both_kernel, places, len(sources), f is not None, planes, group, groups),
        in_specs=[pl.BlockSpec(memory_space=pltpu.SMEM)] + [ANY] * (len(args) - 1),
        out_specs=[ANY] * 3,
        out_shape=[
            jax.ShapeDtypeStruct((pairs, 2, rows, width), F32),
            jax.ShapeDtypeStruct((pairs, 2, total, width), F32),
            TOKEN,
        ],
        scratch_shapes=[
            raw,
            *operand_scratch(rows, total, max(rows, pairs * total)),
            pltpu.VMEM((6, pairs * total, width), BF16),
            pltpu.VMEM((planes, 6, rows, width), BF16),
            pltpu.VMEM((pairs, 2, rows, width), F32),
            pltpu.VMEM((pairs, 2, total, width), F32),
            raw_sems,
            pltpu.SemaphoreType.DMA((1,)),
            pltpu.SemaphoreType.DMA((planes, tiles)),
            pltpu.SemaphoreType.DMA((tiles, pairs)),
            pltpu.SemaphoreType.DMA((tiles, pairs)),
            pltpu.SemaphoreType.DMA((tiles,)),
        ],
        input_output_aliases=aliases,
        compiler_params=pltpu.CompilerParams(vmem_limit_bytes=VMEM_LIMIT),
        cost_estimate=SMALL,
    )(*args)


def more_call(meta, own6, cands, f, partners, shift, group, groups):
    pairs = f_pairs(meta)
    _, rows, width = own6.shape
    planes = width // rows
    total = rows // groups
    tiles = width // TILE
    sources, (places,) = placed([cands])
    raw, raw_sems = fetch_scratch(pairs, total, width, len(places[0]))
    out_specs = [ANY, ANY]
    out_shape = [jax.ShapeDtypeStruct((pairs, 2, rows, width), F32), TOKEN]
    scratch = [raw, *operand_scratch(rows, total, rows), pltpu.VMEM((pairs, 2, rows, width), F32), raw_sems]
    scratch += [pltpu.SemaphoreType.DMA((1,)), pltpu.SemaphoreType.DMA((2 + len(partners), tiles, pairs))]
    if partners:
        out_specs.append(IN_VMEM)
        out_shape.append(jax.ShapeDtypeStruct((pairs, 8, 128), F32))
        scratch.append(pltpu.VMEM((pairs, 2, rows, width), F32))
    args = [meta, own6, *sources, f, *partners]
    return pl.pallas_call(
        functools.partial(more_kernel, places, len(sources), len(partners), planes, shift, group, groups),
        in_specs=[pl.BlockSpec(memory_space=pltpu.SMEM)] + [ANY] * (len(args) - 1),
        out_specs=out_specs,
        out_shape=out_shape,
        scratch_shapes=scratch,
        input_output_aliases={2 + len(sources): 0},
        compiler_params=pltpu.CompilerParams(vmem_limit_bytes=VMEM_LIMIT),
        cost_estimate=SMALL,
    )(*args)


def f_pairs(meta):
    return meta.shape[0] - 3


STEPS = {
    2: (
        ([("z", 0, 0)], [], []),
        ([("z", 0, 1)], [], []),
        ([("x", 0, 0), ("z", 0, 2)], [("own", 0)], []),
        ([("x", 0, 1), ("z", 0, 3)], [], []),
        ([("x", 0, 2)], [], []),
        ([("x", 0, 3), ("z", 1, 0), ("z", 1, 2), ("zy", 1, 1), ("c", 0, 0), ("d", 0, 1)], [("other", 0)], []),
        ([("x", 1, 0), ("z", 1, 3), ("xy", 1, 1), ("xy", 1, 3), ("e", 0, 3)], [("both", 0)], [("z", 1, 1)]),
        ([("x", 1, 2), ("c", 1, 0)], [("both", 1)], []),
        ([("c", 1, 1)], [("more", 0)], []),
    ),
    1: (
        ([("z", 0, 0)], [], []),
        ([("z", 0, 1)], [], []),
        ([("x", 0, 0)], [("own", 0)], []),
        ([("x", 0, 1), ("z", 1, 0), ("zy", 1, 1)], [], []),
        ([("x", 1, 0), ("c", 0, 0), ("xy", 1, 1)], [("other", 0)], []),
        ([("c", 1, 0)], [("both", 0)], []),
    ),
}


def body(fields, offsets):
    own = fields[0]
    pairs = offsets.shape[1]
    _, rows, width = own.shape
    steps = lax.axis_size("tm")
    planes = lax.axis_size("mode")
    me = lax.axis_index("tm")
    lane = lax.rem(me, 2)
    odd_chip = lax.rem(lax.div(me, 2), 2)
    groups = 2 if rows >= 512 else 1
    part = rows // groups // 2

    distance = offsets[0]
    place = jnp.where((lane == 1) & (distance % 2 == 1), 3 - distance, distance - 1)
    meta = jnp.concatenate([place, jnp.stack([lax.axis_index("mode"), odd_chip, lane])]).astype(jnp.int32)
    odd_at, lane_at = pairs + 1, pairs + 2

    def from_later(x):
        return lax.ppermute(x, "tm", [((i + 4) % steps, i) for i in range(steps)])

    def from_plane(x, shift):
        return lax.ppermute(x, "mode", [((i + shift) % planes, i) for i in range(planes)])

    def across_chips(x):
        return lax.ppermute(x, "tm", [(i ^ 2, i) for i in range(steps)])

    def across_cores(x):
        return lax.ppermute(x, "tm", [(i ^ 1, i) for i in range(steps)])

    got = {}

    def here(j, q):
        if j == 0:
            return own, q * part
        return got["y", j], q * part

    fresh = {"e": [("x", 0, 3)], "c": [("x", 1, 0), ("x", 1, 2), ("x", 1, 3)]}

    def piece(user, *name):
        return held(got[name]) if planes == 2 and groups == 2 and name in fresh.get(user, []) else got[name]

    def operand(kind, j, q):
        if kind == "z":
            return [(0, part, None, [here(j, q)])]
        if kind in ("zy", "xy", "e"):
            return [(0, part, None, [(piece(kind, "x" if kind == "e" else kind[0], 0, q), 0)])]
        if kind == "x":
            arrived = held(got["z", j, q]) if planes == 2 else got["z", j, q]
            return [(0, part, odd_at, [(arrived, 0), here(j, q)])]
        pieces = (2 * q, 2 * q + 1)
        pieces_x = pieces[:1] if kind == "d" else pieces
        out = [(i * part, part, None, [(piece(kind, "x", j, p), 0)]) for i, p in enumerate(pieces_x)]
        return out + [
            ((i + len(pieces_x)) * part, part, lane_at, [(piece(kind, "z", j, p), 0), here(j, p)]) for i, p in enumerate(pieces)
        ]

    def send(kind, j, q, x):
        if kind in ("zy", "xy"):
            return from_plane(x, j)
        if kind == "z":
            return from_later(x)
        if kind == "x":
            return across_chips(x)
        return across_cores(x)

    def candidates(j, group, near=False):
        picks = (2 * group, 2 * group + 1)
        if ("c", j, group) in got:
            swapped = held(got["c", j, group]) if near else got["c", j, group]
            cross4 = [(swapped, 2 * part), (swapped, 3 * part)]
            cross2 = [(swapped, 0), (swapped, part)]
        else:
            swapped = got["d", j, group]
            cross4 = [(swapped, part), (swapped, 2 * part)]
            cross2 = [(swapped, 0), (held(got["e", j, picks[1]]), 0)]
        return [
            cross4,
            [(got["x", j, q], 0) for q in picks],
            cross2,
            [(got["z", j, q], 0) for q in picks],
        ]

    f, own6, others6, partners = None, None, [], []

    for j in range(1, planes):
        got["y", j] = from_plane(own, j)
    written = []
    for step, work, there in STEPS[groups]:
        tasks, after = [], list(written[-1:])
        for kind, other, q in step:
            tasks += [(kind, j, q) for j in (range(1, planes) if other else [0])]
        after += [got[kind, j, q] for kind, other, q in there for j in (range(1, planes) if other else [0])]
        for kind, g in work:
            if kind == "own":
                own6, done = split_block(own)
                after.append(done)
            elif kind == "other":
                for j in range(1, planes):
                    block6, done = split_block(got["y", j])
                    others6.append(block6)
                    after.append(done)
            elif kind == "more":
                for j in range(1, planes):
                    f, done = more_call(meta, own6, candidates(j, g), f, [], j, g, groups)
                    after.append(done)
            else:
                f, partner, done = both_call(meta, own6, others6, candidates(0, g), f, g, groups)
                partners.append(partner)
                after.append(done)
        written = route(
            meta, [operand(*task) for task in tasks], after, [planes == 2 and task[0] != "d" for task in tasks]
        )
        for (kind, j, q), x in zip(tasks, written[:-1]):
            got[kind[0], j, q] = send(kind, j, q, x)

    for j in range(1, planes):
        near, last = planes == 2, j == planes - 1
        cands = candidates(j, groups - 1, near)
        out = more_call(meta, own6, cands, f, partners if last else [], j, groups - 1, groups)
        f = out[0]
    partial_trace = jnp.sum(out[2], axis=(1, 2)) / F32(width)
    if planes == 2:
        traces = partial_trace + from_plane(partial_trace, 1)
    else:
        traces = lax.psum(partial_trace, "mode")
    return (f[None], traces[None])


def solution(mesh):
    in_specs = (P("tm", None, "mode", None), P("tm", None))
    out_specs = (P("tm", None, None, "mode", None), P("tm", None))
    return jax.shard_map(body, mesh=mesh, in_specs=in_specs, out_specs=out_specs, check_vma=False)
```

```python
import functools

import jax
import jax.numpy as jnp
from jax import lax
from jax.experimental import pallas as pl
from jax.experimental.pallas import tpu as pltpu
from jax.sharding import PartitionSpec as P

F32 = jnp.float32
BF16 = jnp.bfloat16
VMEM_LIMIT = 54 * 1024 * 1024
ROUTE_LIMIT = 54 * 1024 * 1024
TILE = 512
SPLIT_TILE = 256
CHUNKS = 2
GATE = pl.CostEstimate(flops=1, bytes_accessed=1, transcendentals=0)
SMALL = pl.CostEstimate(flops=1, bytes_accessed=1, transcendentals=0)
TOKEN = jax.ShapeDtypeStruct((8, 128), F32)
ANY = pl.BlockSpec(memory_space=pl.ANY)
IN_VMEM = pl.BlockSpec(memory_space=pltpu.VMEM)


def held(x):
    return pltpu.with_memory_space_constraint(x, pltpu.VMEM)


def route_kernel(plan, chosen, count, *refs):
    meta = refs[0]
    ins, refs = refs[chosen : chosen + count], refs[chosen + count :]
    outs, (_, sems) = refs[: len(plan)], refs[len(plan) :]
    moves = []
    for out, pieces in zip(outs, plan):
        for dst, rows, selector, options in pieces:
            step = rows // CHUNKS
            for c in range(CHUNKS):
                made = [
                    pltpu.make_async_copy(
                        ins[i].at[:, pl.ds(row + c * step, step), :],
                        out.at[:, pl.ds(dst + c * step, step), :],
                        sems.at[len(moves)],
                    )
                    for i, row in options
                ]
                moves.append((selector, made))
    for selector, made in moves:
        if selector is None:
            made[0].start()
        else:
            for value, copy in enumerate(made):
                pl.when(meta[selector] == value)(copy.start)
    for _, made in moves:
        made[0].wait()


def route(meta, outputs, after, near):
    arrays, place = [], {}
    plan = []
    for pieces in outputs:
        listed = []
        for dst, rows, selector, options in pieces:
            numbered = []
            for array, row in options:
                if id(array) not in place:
                    place[id(array)] = len(arrays)
                    arrays.append(array)
                numbered.append((place[id(array)], row))
            listed.append((dst, rows, selector, numbered))
        plan.append(listed)
    width = arrays[0].shape[2]
    heights = [sum(piece[1] for piece in pieces) for pieces in plan]
    arrays += after
    chosen = any(piece[2] is not None for pieces in plan for piece in pieces)
    return pl.pallas_call(
        functools.partial(route_kernel, plan, int(chosen), len(arrays)),
        in_specs=[pl.BlockSpec(memory_space=pltpu.SMEM)] * chosen + [ANY] * len(arrays),
        out_specs=[pl.BlockSpec(memory_space=pltpu.VMEM)] * len(plan) + [ANY],
        out_shape=[
            (pltpu.VMEM if n else jax.ShapeDtypeStruct)((2, h, width), F32) for n, h in zip(near, heights)
        ]
        + [TOKEN],
        scratch_shapes=[pltpu.SemaphoreType.DMA((CHUNKS * sum(len(p) for p in plan),))],
        compiler_params=pltpu.CompilerParams(vmem_limit_bytes=ROUTE_LIMIT),
        cost_estimate=GATE,
    )(*[meta] * chosen, *arrays)


def split(x):
    hi = x.astype(BF16)
    return hi, (x - hi.astype(F32)).astype(BF16)


def parts_of(re, im):
    out = []
    for x in (re, im, re + im):
        out.extend(split(x))
    return out


def split_kernel(x_ref, out, _):
    for index, value in enumerate(parts_of(x_ref[0], x_ref[1])):
        out[index] = value


def split_block(x):
    _, rows, width = x.shape
    return pl.pallas_call(
        split_kernel,
        grid=(width // SPLIT_TILE,),
        in_specs=[pl.BlockSpec((2, rows, SPLIT_TILE), lambda n: (0, 0, n))],
        out_specs=[pl.BlockSpec((6, rows, SPLIT_TILE), lambda n: (0, 0, n)), ANY],
        out_shape=[jax.ShapeDtypeStruct((6, rows, width), BF16), TOKEN],
        compiler_params=pltpu.CompilerParams(vmem_limit_bytes=VMEM_LIMIT),
        cost_estimate=SMALL,
    )(x)


def fetch_start(meta, places, sources, raw, sems, k, t):
    part = raw.shape[2] // len(places[0])
    cols = pl.ds(t * TILE, TILE)
    for c in range(4):

        @pl.when(meta[k] == c)
        def _():
            for p, (index, row) in enumerate(places[c]):
                source = sources[index].at[:, pl.ds(row, part), cols]
                spot = raw.at[k, :, pl.ds(p * part, part), cols]
                pltpu.make_async_copy(source, spot, sems.at[k, p, t]).start()


def fetch_wait(places, raw, sems, k, t, cols):
    part = raw.shape[2] // len(places[0])
    for p in range(len(places[0])):
        spot = raw.at[k, :, pl.ds(p * part, part), cols]
        pltpu.make_async_copy(spot, spot, sems.at[k, p, t]).wait()


def tile_at(t):
    return pl.ds(pl.multiple_of(t * TILE, TILE), TILE)


def own_columns(own6, left6, sem, block, total):
    cols = pl.ds(pl.multiple_of(block * total, total), total)
    return pltpu.make_async_copy(own6.at[:, :, cols], left6, sem.at[0])


def lay_left(left6, left):
    total = left6.shape[2]
    for which in range(3):
        for slot, index in enumerate((2 * which, 2 * which, 2 * which + 1)):
            left[which, :, pl.ds(slot * total, total)] = left6[index]


def lay_right(right, which, high, low):
    total = high.shape[0]
    for slot, value in enumerate((high, low, high)):
        right[which, pl.ds(slot * total, total), :] = value


def products(left, right, sums):
    rows = left.shape[1]
    for which in range(3):
        sums[which, pl.ds(0, rows), :] = jnp.dot(left[which], right[which], preferred_element_type=F32)


def both_kernel(places, count, has_sum, planes, group, groups, meta, own6, *refs):
    sources, refs = refs[:count], refs[count:]
    blocks, refs = (own6, *refs[: planes - 1]), refs[planes - 1 :]
    if has_sum:
        f_in, refs = refs[0], refs[1:]
    f_out, p_out, _, raw, left6, left, *refs = refs
    (rights, sums), (parts, held, f_held, p_held, *sems) = (refs[:2], refs[2:4]), refs[4:]
    raw_sems, left_sem, block_sems, in_sems, out_sems, p_sems = sems
    pairs, _, total, width = raw.shape
    rows = left.shape[1]
    tiles = width // TILE
    plane = meta[pairs]

    def load_sum(t, k):
        spot = (k, slice(None), slice(None), tile_at(t))
        return pltpu.make_async_copy(f_in.at[spot], f_held.at[spot], in_sems.at[t, k])

    def give_sum(t, k):
        spot = (k, slice(None), slice(None), tile_at(t))
        return pltpu.make_async_copy(f_held.at[spot], f_out.at[spot], out_sems.at[t, k])

    def load_block(j, t):
        return pltpu.make_async_copy(blocks[j].at[:, :, tile_at(t)], held.at[j, :, :, tile_at(t)], block_sems.at[j, t])

    def give_partner(t):
        spot = (slice(None), slice(None), slice(None), tile_at(t))
        return pltpu.make_async_copy(p_held.at[spot], p_out.at[spot], p_sems.at[t])

    load_left = own_columns(own6, left6, left_sem, plane * groups + group, total)
    load_left.start()
    for t in range(tiles):
        for k in range(pairs):
            fetch_start(meta, places, sources, raw, raw_sems, k, t)
            if has_sum:
                load_sum(t, k).start()
    for t in range(tiles):
        for j in range(planes):
            load_block(j, t).start()
    load_left.wait()
    lay_left(left6, left)

    def lay(t, k):
        cols, band = tile_at(t), pl.ds(k * total, total)
        fetch_wait(places, raw, raw_sems, k, t, cols)
        re, im = raw[k, 0, :, cols], raw[k, 1, :, cols]
        for which, value in enumerate((re, im, re + im)):
            high, low = split(value)
            lay_right(rights[k % 2], which, high, low)
            parts[2 * which, band, cols] = high
            parts[2 * which + 1, band, cols] = low

    def finish(t, k):
        cols = tile_at(t)
        t0, t1, t2 = (sums[k % 2][which, pl.ds(0, rows), :] for which in range(3))
        fr, fi = t0 - t1, t2 - t0 - t1
        if has_sum:
            fr, fi = fr + f_held[k, 0, :, cols], fi + f_held[k, 1, :, cols]
        f_held[k, 0, :, cols] = fr
        f_held[k, 1, :, cols] = fi

    def forward(t, carry):
        if has_sum:
            for k in range(pairs):
                load_sum(t, k).wait()
        lay(t, 0)
        for k in range(pairs):
            if k + 1 < pairs:
                lay(t, k + 1)
            products(left, rights[k % 2], sums[k % 2])
            if k > 0:
                finish(t, k - 1)
        finish(t, pairs - 1)
        for k in range(pairs):
            give_sum(t, k).start()
        return carry

    lax.fori_loop(0, tiles, forward, 0)

    def partner(t, carry):
        cols = tile_at(t)
        for j in range(planes):
            load_block(j, t).wait()

        for i in range(3):
            term = None
            for j in range(planes):
                at = pl.multiple_of(lax.rem(plane + j, planes) * rows, rows)
                ah, al = parts[2 * i, :, pl.ds(at, rows)], parts[2 * i + 1, :, pl.ds(at, rows)]
                bh, bl = held[j, 2 * i, :, cols], held[j, 2 * i + 1, :, cols]
                for a, b in ((ah, bh), (ah, bl), (al, bh)):
                    more = jnp.dot(a, b, preferred_element_type=F32)
                    term = more if term is None else term + more
            sums[0][i, pl.ds(0, pairs * total), :] = term
        for k in range(pairs):
            t0, t1, t2 = (sums[0][i, pl.ds(k * total, total), :] for i in range(3))
            p_held[k, 0, :, cols] = t0 - t1
            p_held[k, 1, :, cols] = t2 - t0 - t1
        give_partner(t).start()
        return carry

    lax.fori_loop(0, tiles, partner, 0)
    for t in range(tiles):
        for k in range(pairs):
            give_sum(t, k).wait()
        give_partner(t).wait()


def more_kernel(places, count, partners, planes, shift, group, groups, meta, own6, *refs):
    sources, refs = refs[:count], refs[count:]
    f_in, refs = refs[0], refs[1:]
    p_refs, refs = refs[:partners], refs[partners:]
    f_out, _, refs = refs[0], refs[1], refs[2:]
    if partners:
        tr_out, refs = refs[0], refs[1:]
    raw, left6, left, *refs = refs
    (rights, sums), (f_held, raw_sems, left_sem, sems, *p_held) = (refs[:2], refs[2:4]), refs[4:]
    pairs, _, total, width = raw.shape
    rows = left.shape[1]
    tiles = width // TILE

    def load_sum(t, k):
        spot = (k, slice(None), slice(None), tile_at(t))
        return pltpu.make_async_copy(f_in.at[spot], f_held.at[spot], sems.at[0, t, k])

    def give_sum(t, k):
        spot = (k, slice(None), slice(None), tile_at(t))
        return pltpu.make_async_copy(f_held.at[spot], f_out.at[spot], sems.at[1, t, k])

    def load_partners(t, k):
        copies, row = [], 0
        for index, p_ref in enumerate(p_refs):
            high = p_ref.shape[2]
            there = p_held[0].at[k, :, pl.ds(row, high), tile_at(t)]
            copies.append(pltpu.make_async_copy(p_ref.at[k, :, :, tile_at(t)], there, sems.at[2 + index, t, k]))
            row += high
        return copies

    load_left = own_columns(own6, left6, left_sem, lax.rem(meta[pairs] + shift, planes) * groups + group, total)
    load_left.start()
    for t in range(tiles):
        for k in range(pairs):
            fetch_start(meta, places, sources, raw, raw_sems, k, t)
            load_sum(t, k).start()
            for copy in load_partners(t, k):
                copy.start()
    if partners:
        tr_out[...] = jnp.zeros_like(tr_out)
    load_left.wait()
    lay_left(left6, left)

    def lay(t, k):
        cols = tile_at(t)
        fetch_wait(places, raw, raw_sems, k, t, cols)
        re, im = raw[k, 0, :, cols], raw[k, 1, :, cols]
        for which, value in enumerate((re, im, re + im)):
            lay_right(rights[k % 2], which, *split(value))

    def finish(t, k):
        cols = tile_at(t)
        t0, t1, t2 = (sums[k % 2][which, pl.ds(0, rows), :] for which in range(3))
        fr, fi = t0 - t1 + f_held[k, 0, :, cols], t2 - t0 - t1 + f_held[k, 1, :, cols]
        f_held[k, 0, :, cols] = fr
        f_held[k, 1, :, cols] = fi
        if partners:
            term = fr * p_held[0][k, 0, :, cols] + fi * p_held[0][k, 1, :, cols]
            term = jnp.sum(term.reshape(rows // 8, 8, TILE), axis=0)
            tr_out[k] += sum(term[:, c * 128 : (c + 1) * 128] for c in range(TILE // 128))

    def forward(t, carry):
        lay(t, 0)
        for k in range(pairs):
            load_sum(t, k).wait()
            for copy in load_partners(t, k):
                copy.wait()
            if k + 1 < pairs:
                lay(t, k + 1)
            products(left, rights[k % 2], sums[k % 2])
            if k > 0:
                finish(t, k - 1)
        finish(t, pairs - 1)
        for k in range(pairs):
            give_sum(t, k).start()
        return carry

    lax.fori_loop(0, tiles, forward, 0)
    for t in range(tiles):
        for k in range(pairs):
            give_sum(t, k).wait()


def placed(groups_of_cands):
    sources, places = [], []
    for cands in groups_of_cands:
        listed = []
        for pieces in cands:
            entry = []
            for array, row in pieces:
                known = [i for i, s in enumerate(sources) if s is array]
                if not known:
                    sources.append(array)
                entry.append((known[0] if known else len(sources) - 1, row))
            listed.append(entry)
        places.append(listed)
    return sources, places


def fetch_scratch(pairs, total, width, pieces):
    return pltpu.VMEM((pairs, 2, total, width), F32), pltpu.SemaphoreType.DMA((pairs, pieces, width // TILE))


def operand_scratch(rows, total, high):
    return [
        pltpu.VMEM((6, rows, total), BF16),
        pltpu.VMEM((3, rows, 3 * total), BF16),
        *[pltpu.VMEM((3, 3 * total, TILE), BF16)] * 2,
        *[pltpu.VMEM((3, high, TILE), F32)] * 2,
    ]


def both_call(meta, own6, others6, cands, f, group, groups):
    pairs = f_pairs(meta)
    planes = 1 + len(others6)
    _, rows, width = own6.shape
    total = rows // groups
    tiles = width // TILE
    sources, (places,) = placed([cands])
    raw, raw_sems = fetch_scratch(pairs, total, width, len(places[0]))
    args = [meta, own6, *sources, *others6]
    aliases = {}
    if f is not None:
        aliases = {len(args): 0}
        args.append(f)
    return pl.pallas_call(
        functools.partial(both_kernel, places, len(sources), f is not None, planes, group, groups),
        in_specs=[pl.BlockSpec(memory_space=pltpu.SMEM)] + [ANY] * (len(args) - 1),
        out_specs=[ANY] * 3,
        out_shape=[
            jax.ShapeDtypeStruct((pairs, 2, rows, width), F32),
            jax.ShapeDtypeStruct((pairs, 2, total, width), F32),
            TOKEN,
        ],
        scratch_shapes=[
            raw,
            *operand_scratch(rows, total, max(rows, pairs * total)),
            pltpu.VMEM((6, pairs * total, width), BF16),
            pltpu.VMEM((planes, 6, rows, width), BF16),
            pltpu.VMEM((pairs, 2, rows, width), F32),
            pltpu.VMEM((pairs, 2, total, width), F32),
            raw_sems,
            pltpu.SemaphoreType.DMA((1,)),
            pltpu.SemaphoreType.DMA((planes, tiles)),
            pltpu.SemaphoreType.DMA((tiles, pairs)),
            pltpu.SemaphoreType.DMA((tiles, pairs)),
            pltpu.SemaphoreType.DMA((tiles,)),
        ],
        input_output_aliases=aliases,
        compiler_params=pltpu.CompilerParams(vmem_limit_bytes=VMEM_LIMIT),
        cost_estimate=SMALL,
    )(*args)


def more_call(meta, own6, cands, f, partners, shift, group, groups):
    pairs = f_pairs(meta)
    _, rows, width = own6.shape
    planes = width // rows
    total = rows // groups
    tiles = width // TILE
    sources, (places,) = placed([cands])
    raw, raw_sems = fetch_scratch(pairs, total, width, len(places[0]))
    out_specs = [ANY, ANY]
    out_shape = [jax.ShapeDtypeStruct((pairs, 2, rows, width), F32), TOKEN]
    scratch = [raw, *operand_scratch(rows, total, rows), pltpu.VMEM((pairs, 2, rows, width), F32), raw_sems]
    scratch += [pltpu.SemaphoreType.DMA((1,)), pltpu.SemaphoreType.DMA((2 + len(partners), tiles, pairs))]
    if partners:
        out_specs.append(IN_VMEM)
        out_shape.append(jax.ShapeDtypeStruct((pairs, 8, 128), F32))
        scratch.append(pltpu.VMEM((pairs, 2, rows, width), F32))
    args = [meta, own6, *sources, f, *partners]
    return pl.pallas_call(
        functools.partial(more_kernel, places, len(sources), len(partners), planes, shift, group, groups),
        in_specs=[pl.BlockSpec(memory_space=pltpu.SMEM)] + [ANY] * (len(args) - 1),
        out_specs=out_specs,
        out_shape=out_shape,
        scratch_shapes=scratch,
        input_output_aliases={2 + len(sources): 0},
        compiler_params=pltpu.CompilerParams(vmem_limit_bytes=VMEM_LIMIT),
        cost_estimate=SMALL,
    )(*args)


def f_pairs(meta):
    return meta.shape[0] - 3


STEPS = {
    2: (
        ([("z", 0, 0)], [], []),
        ([("z", 0, 1)], [], []),
        ([("x", 0, 0), ("z", 0, 2)], [("own", 0)], []),
        ([("x", 0, 1), ("z", 0, 3)], [], []),
        ([("x", 0, 2)], [], []),
        ([("x", 0, 3), ("z", 1, 0), ("z", 1, 2), ("zy", 1, 1), ("c", 0, 0), ("d", 0, 1)], [("other", 0)], []),
        ([("x", 1, 0), ("z", 1, 3), ("xy", 1, 1), ("xy", 1, 3), ("e", 0, 3)], [("both", 0)], [("z", 1, 1)]),
        ([("x", 1, 2), ("c", 1, 0)], [("both", 1)], []),
        ([("c", 1, 1)], [("more", 0)], []),
    ),
    1: (
        ([("z", 0, 0)], [], []),
        ([("z", 0, 1)], [], []),
        ([("x", 0, 0)], [("own", 0)], []),
        ([("x", 0, 1), ("z", 1, 0), ("zy", 1, 1)], [], []),
        ([("x", 1, 0), ("c", 0, 0), ("xy", 1, 1)], [("other", 0)], []),
        ([("c", 1, 0)], [("both", 0)], []),
    ),
}


def body(fields, offsets):
    own = fields[0]
    pairs = offsets.shape[1]
    _, rows, width = own.shape
    steps = lax.axis_size("tm")
    planes = lax.axis_size("mode")
    me = lax.axis_index("tm")
    lane = lax.rem(me, 2)
    odd_chip = lax.rem(lax.div(me, 2), 2)
    groups = 2 if rows >= 512 else 1
    part = rows // groups // 2

    distance = offsets[0]
    place = jnp.where((lane == 1) & (distance % 2 == 1), 3 - distance, distance - 1)
    meta = jnp.concatenate([place, jnp.stack([lax.axis_index("mode"), odd_chip, lane])]).astype(jnp.int32)
    odd_at, lane_at = pairs + 1, pairs + 2

    def from_later(x):
        return lax.ppermute(x, "tm", [((i + 4) % steps, i) for i in range(steps)])

    def from_plane(x, shift):
        return lax.ppermute(x, "mode", [((i + shift) % planes, i) for i in range(planes)])

    def across_chips(x):
        return lax.ppermute(x, "tm", [(i ^ 2, i) for i in range(steps)])

    def across_cores(x):
        return lax.ppermute(x, "tm", [(i ^ 1, i) for i in range(steps)])

    got = {}

    def here(j, q):
        if j == 0:
            return own, q * part
        return got["y", j], q * part

    fresh = {"e": [("x", 0, 3)], "c": [("x", 1, 0), ("x", 1, 2), ("x", 1, 3)]}

    def piece(user, *name):
        return held(got[name]) if planes == 2 and groups == 2 and name in fresh.get(user, []) else got[name]

    def operand(kind, j, q):
        if kind == "z":
            return [(0, part, None, [here(j, q)])]
        if kind in ("zy", "xy", "e"):
            return [(0, part, None, [(piece(kind, "x" if kind == "e" else kind[0], 0, q), 0)])]
        if kind == "x":
            arrived = held(got["z", j, q]) if planes == 2 else got["z", j, q]
            return [(0, part, odd_at, [(arrived, 0), here(j, q)])]
        pieces = (2 * q, 2 * q + 1)
        pieces_x = pieces[:1] if kind == "d" else pieces
        out = [(i * part, part, None, [(piece(kind, "x", j, p), 0)]) for i, p in enumerate(pieces_x)]
        return out + [
            ((i + len(pieces_x)) * part, part, lane_at, [(piece(kind, "z", j, p), 0), here(j, p)]) for i, p in enumerate(pieces)
        ]

    def send(kind, j, q, x):
        if kind in ("zy", "xy"):
            return from_plane(x, j)
        if kind == "z":
            return from_later(x)
        if kind == "x":
            return across_chips(x)
        return across_cores(x)

    def candidates(j, group, near=False):
        picks = (2 * group, 2 * group + 1)
        if ("c", j, group) in got:
            swapped = held(got["c", j, group]) if near else got["c", j, group]
            cross4 = [(swapped, 2 * part), (swapped, 3 * part)]
            cross2 = [(swapped, 0), (swapped, part)]
        else:
            swapped = got["d", j, group]
            cross4 = [(swapped, part), (swapped, 2 * part)]
            cross2 = [(swapped, 0), (held(got["e", j, picks[1]]), 0)]
        return [
            cross4,
            [(got["x", j, q], 0) for q in picks],
            cross2,
            [(got["z", j, q], 0) for q in picks],
        ]

    f, own6, others6, partners = None, None, [], []

    for j in range(1, planes):
        got["y", j] = from_plane(own, j)
    written = []
    for step, work, there in STEPS[groups]:
        tasks, after = [], list(written[-1:])
        for kind, other, q in step:
            tasks += [(kind, j, q) for j in (range(1, planes) if other else [0])]
        waited = [got[kind, j, q] for kind, other, q in there for j in (range(1, planes) if other else [0])]
        after += [held(x) for x in waited] if planes == 2 else waited
        for kind, g in work:
            if kind == "own":
                own6, done = split_block(own)
                after.append(done)
            elif kind == "other":
                for j in range(1, planes):
                    block6, done = split_block(got["y", j])
                    others6.append(block6)
                    after.append(done)
            elif kind == "more":
                for j in range(1, planes):
                    f, done = more_call(meta, own6, candidates(j, g), f, [], j, g, groups)
                    after.append(done)
            else:
                f, partner, done = both_call(meta, own6, others6, candidates(0, g), f, g, groups)
                partners.append(partner)
                after.append(done)
        written = route(
            meta, [operand(*task) for task in tasks], after, [planes == 2 and task[0] != "d" for task in tasks]
        )
        for (kind, j, q), x in zip(tasks, written[:-1]):
            got[kind[0], j, q] = send(kind, j, q, x)

    for j in range(1, planes):
        near, last = planes == 2, j == planes - 1
        cands = candidates(j, groups - 1, near)
        out = more_call(meta, own6, cands, f, partners if last else [], j, groups - 1, groups)
        f = out[0]
    partial_trace = jnp.sum(out[2], axis=(1, 2)) / F32(width)
    if planes == 2:
        traces = partial_trace + from_plane(partial_trace, 1)
    else:
        traces = lax.psum(partial_trace, "mode")
    return (f[None], traces[None])


def solution(mesh):
    in_specs = (P("tm", None, "mode", None), P("tm", None))
    out_specs = (P("tm", None, None, "mode", None), P("tm", None))
    return jax.shard_map(body, mesh=mesh, in_specs=in_specs, out_specs=out_specs, check_vma=False)
```
